256 devices in a mesh: leaf: 128 (over y, z, x), sub: 2 (over core).
Axes of the slice: x: 4, y: 4, z: 8, core: 2. Of those that a mesh axis runs over, the one named last changes fastest.
Arguments:
- coords: float32 [3, 2097152], P(None, ('leaf', 'sub')), may hold values from 0 to 1
- vectors: bfloat16 [2097152, 64], P(('leaf', 'sub')), may hold values from -6 to 6
- bases: bfloat16 [32768, 64, 64], P(('leaf', 'sub')), may hold values from -0.75 to 0.75
- transfer: bfloat16 [256, 254, 64, 64], P(('leaf', 'sub')), may hold values from -0.5234375 to 0.5234375
- coupling: bfloat16 [256, 31, 64, 64], P(('leaf', 'sub')), may hold values from -0.75 to 0.75
- top_transfer: bfloat16 [508, 64, 64], replicated, may hold values from -0.5234375 to 0.5234375
- top_coupling: bfloat16 [255, 64, 64], replicated, may hold values from -0.75 to 0.75
Outputs:
- product: float32 [2097152, 64], P(('leaf', 'sub'))
The draws below stay inside these ranges and needn't reach their ends.
All inputs are finite; a program needn't handle non-finite values.
Results may differ from the reference program's by a relative error of at most 0.0029.
Values sent between devices are 32-bit elements; how exact they have to be, the bound alone decides.
No kernel may reach another device: no remote copies, remote signals or barrier semaphores. Data moves between devices by JAX's collectives and lax.ppermute only.
A program may use at most 128 MiB of HBM per device.

```python
import jax
import jax.numpy as jnp
from jax import lax

P_SIZE = 64
K = 64
V = 64
NEAR_LEAVES = 4
DEVS = 256
LEAVES = 32768
NPTS = 2097152
NODES_DEV = 254
COUPLE_DEV = 31
TOP_TRANS = 508
TOP_PAIRS = 255


def shard_levels(stream_key, shape, shards, least, top_value):
    level = 1.0
    for position, parts in shards:
        steps = jax.random.uniform(jax.random.fold_in(jax.random.fold_in(stream_key, 6), position), (parts,), jnp.float32, least / len(shards), top_value / len(shards))
        level = level * jnp.repeat(jnp.exp(steps), shape[position] // parts).reshape((-1,) + (1,) * (len(shape) - 1 - position))
    return level


def noise(own_key, dims, spread, bound, pieces=(), kind=jnp.bfloat16):
    entries = spread * jax.random.normal(own_key, dims, jnp.float32)
    if pieces:
        entries = entries * shard_levels(own_key, dims, pieces, -0.22, 0.18)
    return jnp.clip(entries, -bound, bound).astype(kind)


def setup_inputs(seed: int = 0) -> dict:
    key_list = jax.random.split(jax.random.key(seed), 8)
    coords = jnp.clip(1.0 * jax.random.uniform(key_list[0], (3, NPTS), jnp.float32) ** shard_levels(key_list[0], (3, NPTS), ((1, 256),), -0.2, 0.2), 0.0, 1.0)
    vectors = noise(key_list[1], (NPTS, V), 1.0, 6.0, ((0, 256),))
    bases = noise(key_list[2], (LEAVES, P_SIZE, K), P_SIZE ** -0.5, 0.75, ((0, 256),))
    transfer = noise(key_list[3], (DEVS, NODES_DEV, K, K), (0.8409 * K ** -0.5), 0.5234375, ((0, 256),))
    coupling = noise(key_list[4], (DEVS, COUPLE_DEV, K, K), K ** -0.5, 0.75, ((0, 256),))
    top_transfer = noise(key_list[5], (TOP_TRANS, K, K), (0.8409 * K ** -0.5), 0.5234375)
    top_coupling = noise(key_list[6], (TOP_PAIRS, K, K), K ** -0.5, 0.75)
    return {"coords": coords, "vectors": vectors, "bases": bases, "transfer": transfer, "coupling": coupling, "top_transfer": top_transfer, "top_coupling": top_coupling}


VARIANCE = 1.0
LENGTH_SCALE = 0.5
NUGGET = 0.5
HIGH_ACCURACY = lax.Precision.HIGHEST

def near_apply(points, values):
    groups = points.shape[1]
    width = points.shape[2]
    square = jnp.zeros((groups, width, width), jnp.float32)
    for axis_id in range(3):
        column = points[axis_id]
        offset = column[:, :, None] - column[:, None, :]
        square = square + offset * offset
    distance = jnp.sqrt(square)
    identity = jnp.eye(width, dtype=jnp.float32)
    matern_kernel = VARIANCE * jnp.exp(-distance / LENGTH_SCALE) + NUGGET * identity
    matern_kernel = lax.optimization_barrier(matern_kernel.astype(jnp.bfloat16)).astype(jnp.float32)
    return jnp.einsum('grs,gsv->grv', matern_kernel, values.astype(jnp.float32))

def couple(pairs, expansion_weights):
    even_part = expansion_weights[0::2]
    odd_part = expansion_weights[1::2]
    to_even = jnp.einsum('pkj,pjv->pkv', pairs, odd_part, precision=HIGH_ACCURACY)
    to_odd = jnp.einsum('pjk,pjv->pkv', pairs, even_part, precision=HIGH_ACCURACY)
    return jnp.stack([to_even, to_odd], axis=1).reshape(expansion_weights.shape)

def lift(transfer_matrix, expansion_weights):
    projected_values = jnp.einsum('lhm,lhc->lmc', transfer_matrix, expansion_weights, precision=HIGH_ACCURACY)
    return projected_values[0::2] + projected_values[1::2]

def lower(transfer_matrix, parent_node):
    return jnp.einsum('dea,dab->deb', transfer_matrix, jnp.repeat(parent_node, 2, axis=0), precision=HIGH_ACCURACY)

def up_local(base_dev, vec_dev, trans_dev, couple_dev):
    leaves = base_dev.shape[0]
    height_top = leaves.bit_length() - 1
    first = NEAR_LEAVES.bit_length() - 1
    values = vec_dev.reshape(leaves, base_dev.shape[1], -1)
    current = jnp.einsum('lpk,lpv->lkv', base_dev.astype(jnp.float32), values.astype(jnp.float32))
    fields = []
    trans_off = 0
    pair_off = 0
    for height in range(height_top):
        count = current.shape[0]
        if height >= first:
            pairs = couple_dev[pair_off:pair_off + count // 2].astype(jnp.float32)
            fields.append(couple(pairs, current))
            pair_off += count // 2
        transfer_matrix = trans_dev[trans_off:trans_off + count].astype(jnp.float32)
        trans_off += count
        current = lift(transfer_matrix, current)
    return (current[0], tuple(fields))

def down_local(going, fields, base_dev, vec_dev, coord_dev, trans_dev):
    leaves = base_dev.shape[0]
    height_top = leaves.bit_length() - 1
    first = NEAR_LEAVES.bit_length() - 1
    current = going[None]
    trans_off = trans_dev.shape[0]
    for height in range(height_top - 1, -1, -1):
        count = leaves >> height
        trans_off -= count
        transfer_matrix = trans_dev[trans_off:trans_off + count].astype(jnp.float32)
        current = lower(transfer_matrix, current)
        if height >= first:
            current = current + fields[height - first]
    rounded = lax.optimization_barrier(current.astype(jnp.bfloat16)).astype(jnp.float32)
    far_part = jnp.einsum('lpk,lkv->lpv', base_dev.astype(jnp.float32), rounded)
    groups = leaves // NEAR_LEAVES
    width = NEAR_LEAVES * base_dev.shape[1]
    near_part = near_apply(coord_dev.reshape(3, groups, width), vec_dev.reshape(groups, width, -1))
    return far_part.reshape(leaves * base_dev.shape[1], -1) + near_part.reshape(leaves * base_dev.shape[1], -1)

def top_pass(dev_coefs, top_transfer, top_coupling):
    devs = dev_coefs.shape[0]
    levels = devs.bit_length() - 1
    current = dev_coefs
    fields = []
    for height in range(levels):
        count = current.shape[0]
        start = devs - count
        pairs = top_coupling[start:start + count // 2].astype(jnp.float32)
        fields.append(couple(pairs, current))
        if height < levels - 1:
            tstart = 2 * (devs - count)
            current = lift(top_transfer[tstart:tstart + count].astype(jnp.float32), current)
    going = fields[-1]
    for height in range(levels - 2, -1, -1):
        count = devs >> height
        tstart = 2 * (devs - count)
        going = fields[height] + lower(top_transfer[tstart:tstart + count].astype(jnp.float32), going)
    return going

def reference(coords, vectors, bases, transfer, coupling, top_transfer, top_coupling):
    devs = transfer.shape[0]
    leaves_dev = bases.shape[0] // devs
    points = bases.shape[1]
    npts_dev = leaves_dev * points
    coord_all = coords.reshape(3, devs, npts_dev).transpose(1, 0, 2)
    vec_all = vectors.reshape(devs, npts_dev, vectors.shape[1])
    base_all = bases.reshape(devs, leaves_dev, points, bases.shape[2])

    def upward(items):
        return up_local(items[0], items[1], items[2], items[3])
    dev_coefs, fields = lax.map(upward, (base_all, vec_all, transfer, coupling))
    going = top_pass(dev_coefs, top_transfer, top_coupling)

    def downward(items):
        return down_local(items[0], items[1], items[2], items[3], items[4], items[5])
    result = lax.map(downward, (going, fields, base_all, vec_all, coord_all, transfer))
    return result.reshape(devs * npts_dev, vectors.shape[1])
```

```python
import functools

import jax
import jax.numpy as jnp
from jax import lax
from jax.experimental import pallas as pl
from jax.experimental.pallas import tpu as pltpu
from jax.sharding import PartitionSpec as P

F32 = jnp.float32
BF16 = jnp.bfloat16
VMEM = pltpu.VMEM
AXES = ("leaf", "sub")
HIGH = lax.Precision.HIGHEST

STEP = 136
NN = (((1,), (0,)), ((), ()))
NT = (((1,), (1,)), ((), ()))
TN = (((0,), (0,)), ((), ()))
LEVEL_AT = (None, 0, 4096, 6144, 7168, 7680, 7936)
NODE_AT = (0, 128, 192, 224, 240, 248, 252)
NUGGET_DIAG = 1.5
CHORD = 2.0 * 1.4426950408889634


def mxu(a, b, dims):
    return lax.dot_general(a, b, dims, preferred_element_type=F32)


def split(c):
    hi = c.astype(BF16)
    lo = (c - hi.astype(F32)).astype(BF16)
    return jnp.concatenate([hi, lo], 0)


def fold(t):
    half = t.shape[0] // 2
    return t[:half] + t[half:]


def picker(bit):
    row = lax.broadcasted_iota(jnp.int32, (128, 256), 0)
    col = lax.broadcasted_iota(jnp.int32, (128, 256), 1)
    return jnp.where(col == row + 128 * ((row >> bit) & 1), 1.0, 0.0).astype(BF16)


def spread(src, width, lane0, pick, slab):
    for i in range(32):
        parts = []
        for u in range(2):
            w = src[2 * i + u, :, lane0 : lane0 + width]
            if width < 128:
                w = jnp.concatenate([w, jnp.zeros((64, 128 - width), BF16)], 1)
            z = jnp.zeros_like(w)
            parts += [jnp.concatenate([w, z], 1), jnp.concatenate([z, w], 1)]
        out = mxu(pick, jnp.concatenate(parts, 0), NT)
        for u in range(2):
            slab[pl.ds((2 * i + u) * STEP, 128), :] = out[:, 128 * u : 128 * u + 128]


def box_matrix(slab, box):
    return slab[pl.ds(box, 64, stride=STEP), :]


def up_kernel(
    bases_h, vectors_h, transfer_h, own_out, levels_h, pairs_h, quads_h,
    bases, vectors, transfer, slab0, slab1, leaf_coef, levels, pairs, quads, sems,
):
    loads = [
        pltpu.make_async_copy(a, b, sems.at[i])
        for i, (a, b) in enumerate(
            [(bases_h, bases), (vectors_h, vectors), (transfer_h, transfer)]
        )
    ]
    for copy in loads:
        copy.start()
    pick_pair = picker(0)
    pick_quad = picker(1)
    loads[0].wait()
    spread(bases, 128, 0, pick_pair, slab0)
    loads[1].wait()
    for j in range(64):
        pair = jnp.concatenate(
            [box_matrix(slab0, 2 * j), box_matrix(slab0, 2 * j + 1)], 0
        ).astype(BF16)
        pairs[j] = pair
        leaf_coef[:, 128 * j : 128 * j + 128] = mxu(
            vectors[:, 128 * j : 128 * j + 128], pair, NN
        )
    store_pairs = pltpu.make_async_copy(pairs, pairs_h, sems.at[3])
    store_pairs.start()
    loads[2].wait()
    spread(transfer, 128, 0, pick_quad, slab1)
    spread(transfer, 126, 128, pick_quad, slab0)
    for level in range(6):
        count = 128 >> level
        for q in range(count // 4):
            first = NODE_AT[level] + 4 * q
            slab = slab1 if first < 128 else slab0
            quad = jnp.concatenate(
                [box_matrix(slab, (first + u) % 128) for u in range(4)], 0
            ).astype(BF16)
            quads[first // 4] = quad
            if level == 0:
                coef = leaf_coef[:, 256 * q : 256 * q + 256]
            else:
                at = LEVEL_AT[level] + 256 * q
                coef = levels[:, at : at + 256]
            at = LEVEL_AT[level + 1] + 128 * q
            levels[:, at : at + 128] = fold(mxu(split(coef), quad, NN))
    last = jnp.concatenate([box_matrix(slab0, 124), box_matrix(slab0, 125)], 0).astype(BF16)
    quads[63, :128, :] = last
    quads[63, 128:, :] = jnp.zeros((128, 128), BF16)
    store_levels = pltpu.make_async_copy(levels, levels_h, sems.at[4])
    store_quads = pltpu.make_async_copy(quads, quads_h, sems.at[5])
    store_levels.start()
    store_quads.start()
    at = LEVEL_AT[6]
    own_out[...] = fold(mxu(split(levels[:, at : at + 128]), last, NN))[:, :64]
    store_pairs.wait()
    store_levels.wait()
    store_quads.wait()


def upward(bases, vectors, transfer):
    return pl.pallas_call(
        up_kernel,
        out_shape=[
            jax.ShapeDtypeStruct((64, 64), F32),
            jax.ShapeDtypeStruct((64, 8064), F32),
            jax.ShapeDtypeStruct((64, 128, 128), BF16),
            jax.ShapeDtypeStruct((64, 256, 128), BF16),
        ],
        in_specs=[pl.BlockSpec(memory_space=pl.ANY)] * 3,
        out_specs=[pl.BlockSpec(memory_space=VMEM)] + [pl.BlockSpec(memory_space=pl.ANY)] * 3,
        scratch_shapes=[
            VMEM((64, 64, 128), BF16),
            VMEM((64, 8192), BF16),
            VMEM((64, 64, 254), BF16),
            VMEM((64 * STEP, 128), F32),
            VMEM((64 * STEP, 128), F32),
            VMEM((64, 8192), F32),
            VMEM((64, 8064), F32),
            VMEM((64, 128, 128), BF16),
            VMEM((64, 256, 128), BF16),
            pltpu.SemaphoreType.DMA((6,)),
        ],
        compiler_params=pltpu.CompilerParams(vmem_limit_bytes=58 * 2**20),
        cost_estimate=pl.CostEstimate(flops=10**9, bytes_accessed=8 * 2**20, transcendentals=0),
        name="upward",
    )(bases, vectors, transfer)


def top_kernel(device, transfer, coupling, own_out, sib_out, fields_out, slab, slab2):
    dev = device[0]
    row = lax.broadcasted_iota(jnp.int32, (16, 508), 0)
    col = lax.broadcasted_iota(jnp.int32, (16, 508), 1)
    height = row & 7
    want = 512 - (512 >> height) + (jnp.full_like(row, dev) >> height)
    want = jnp.where(row >= 8, want ^ 1, want)
    pick = jnp.where((col == want) & (height < 7), 1.0, 0.0).astype(BF16)
    crow = lax.broadcasted_iota(jnp.int32, (16, 255), 0)
    ccol = lax.broadcasted_iota(jnp.int32, (16, 255), 1)
    cwant = 256 - (256 >> crow) + (jnp.full_like(crow, dev) >> (crow + 1))
    cpick = jnp.where((ccol == cwant) & (crow < 8), 1.0, 0.0).astype(BF16)
    for i in range(64):
        slab[pl.ds(i * 24, 16), :64] = mxu(pick, transfer[i], NT)
        slab2[pl.ds(i * 24, 16), :64] = mxu(cpick, coupling[i], NT)
    chain = None
    for level in range(8):
        pair = slab2[pl.ds(level, 64, stride=24), :][:, :64]
        odd = (dev >> level) & 1
        turned = jnp.where(odd == 1, pair, pair.T).astype(BF16)
        if level == 0:
            fields_out[0] = turned.astype(F32)
        else:
            hi = chain.astype(BF16)
            lo = (chain - hi.astype(F32)).astype(BF16)
            fields_out[level] = mxu(turned, hi, NN) + mxu(turned, lo, NN)
        if level < 7:
            own = slab[pl.ds(level, 64, stride=24), :][:, :64]
            own_out[level] = own
            sib_out[level] = slab[pl.ds(level + 8, 64, stride=24), :][:, :64]
            turned_own = own.T
            if level == 0:
                chain = turned_own
            else:
                e = turned_own.astype(BF16)
                chain = mxu(e, hi, NN) + mxu(e, lo, NN)


def top_matrices(device, transfer, coupling):
    return pl.pallas_call(
        top_kernel,
        out_shape=[
            jax.ShapeDtypeStruct((7, 64, 64), F32),
            jax.ShapeDtypeStruct((7, 64, 64), F32),
            jax.ShapeDtypeStruct((8, 64, 64), F32),
        ],
        in_specs=[
            pl.BlockSpec(memory_space=pltpu.SMEM),
            pl.BlockSpec(memory_space=VMEM),
            pl.BlockSpec(memory_space=VMEM),
        ],
        out_specs=[pl.BlockSpec(memory_space=VMEM)] * 3,
        scratch_shapes=[VMEM((64 * 24, 128), F32), VMEM((64 * 24, 128), F32)],
        compiler_params=pltpu.CompilerParams(vmem_limit_bytes=32 * 2**20),
        cost_estimate=pl.CostEstimate(flops=10**9, bytes_accessed=8 * 2**20, transcendentals=0),
        name="top_matrices",
    )(device, transfer, coupling)


def thirds(x):
    a = x.astype(BF16).astype(F32)
    b = (x - a).astype(BF16).astype(F32)
    return a, b, x - a - b


def near_kernel(groups, first, coords, vectors, out):
    eye = (
        lax.broadcasted_iota(jnp.int32, (128, 128), 0)
        == lax.broadcasted_iota(jnp.int32, (128, 128), 1)
    )
    five = jnp.zeros((5, 256), F32)
    one8 = jnp.where(lax.broadcasted_iota(jnp.int32, (8, 256), 0) == 0, 1.0, 0.0)
    for g in range(groups):
        at = 256 * (first + g)
        xyz = coords[:, at : at + 256] * CHORD
        x = jnp.concatenate([xyz, five], 0)
        x1, x2, x3 = thirds(x)
        norm = jnp.sum(x * x, axis=0, keepdims=True) * one8
        n1, n2, n3 = thirds(norm)
        left = jnp.concatenate([x1, x1, x2, x2, x1, x3, n1, n2, n3, one8, one8, one8], 0)
        right = jnp.concatenate(
            [-2 * x1, -2 * x2, -2 * x1, -2 * x2, -2 * x3, -2 * x1, one8, one8, one8, n1, n2, n3], 0
        )
        left_t = left.T.astype(BF16)
        right = right.astype(BF16)

        def kernel_block(a, b):
            square = mxu(left_t[128 * a : 128 * a + 128], right[:, 128 * b : 128 * b + 128], NN)
            square = jnp.maximum(square, 1e-30)
            value = jnp.exp2(-(square * lax.rsqrt(square)))
            if a == b:
                value = jnp.where(eye, NUGGET_DIAG, value)
            return value.astype(BF16)

        v0 = vectors[:, at : at + 128]
        v1 = vectors[:, at + 128 : at + 256]
        side = kernel_block(0, 1)
        out[:, 256 * g : 256 * g + 128] = mxu(v0, kernel_block(0, 0), NN) + mxu(v1, side, NT)
        out[:, 256 * g + 128 : 256 * g + 256] = mxu(v0, side, NN) + mxu(v1, kernel_block(1, 1), NN)


def near(coords, vectors, first, groups):
    return pl.pallas_call(
        functools.partial(near_kernel, groups, first),
        out_shape=jax.ShapeDtypeStruct((64, 256 * groups), F32),
        in_specs=[pl.BlockSpec(memory_space=VMEM)] * 2,
        out_specs=pl.BlockSpec(memory_space=VMEM),
        compiler_params=pltpu.CompilerParams(vmem_limit_bytes=32 * 2**20),
        cost_estimate=pl.CostEstimate(
            flops=groups * 10**8, bytes_accessed=groups * 2**18, transcendentals=groups * 2 * 65536
        ),
        name="near",
    )(coords, vectors)


def down_kernel(pieces, top, coupling, levels, quads, pairs, *refs):
    nears = refs[:pieces]
    out_h = refs[pieces]
    going, shifted, out, sems = refs[pieces + 1 :]
    shift = jnp.where(
        lax.broadcasted_iota(jnp.int32, (64, 128), 1)
        == lax.broadcasted_iota(jnp.int32, (64, 128), 0) + 64,
        1.0,
        0.0,
    ).astype(BF16)
    for p in range(31):
        shifted[64 * p : 64 * p + 64, :] = mxu(coupling[p], shift, NN).astype(BF16)
    blank = jnp.zeros((64, 128), BF16)

    def field(level, pair):
        base = 32 - (32 >> (level - 2))
        s = split(levels[:, LEVEL_AT[level] + 128 * pair : LEVEL_AT[level] + 128 * pair + 128])
        z = jnp.concatenate([shifted[64 * (base + pair) : 64 * (base + pair) + 64, :], blank], 0)
        return fold(mxu(s, z, NN) + mxu(s, z, NT))

    at = LEVEL_AT[6]
    s = split(jnp.concatenate([top[...], jnp.zeros((64, 64), F32)], 1))
    going[:, at : at + 128] = fold(mxu(s, quads[63, :128, :], NT)) + field(6, 0)
    for level in range(5, 0, -1):
        count = 128 >> level
        for q in range(count // 4):
            above = LEVEL_AT[level + 1] + 128 * q
            s = split(going[:, above : above + 128])
            g = fold(mxu(s, quads[NODE_AT[level] // 4 + q], NT))
            at = LEVEL_AT[level] + 256 * q
            if level >= 2:
                g = g + jnp.concatenate([field(level, 2 * q), field(level, 2 * q + 1)], 1)
            going[:, at : at + 256] = g
    copies = []
    width = 8192 // pieces
    for q in range(32):
        above = LEVEL_AT[1] + 128 * q
        s = split(going[:, above : above + 128])
        g = fold(mxu(s, quads[q], NT)).astype(BF16)
        for u in range(2):
            at = 256 * q + 128 * u
            piece, local = divmod(at, width)
            out[:, at : at + 128] = (
                mxu(g[:, 128 * u : 128 * u + 128], pairs[2 * q + u], NT)
                + nears[piece][:, local : local + 128]
            )
        if q % 8 == 7:
            part = pl.ds(256 * (q - 7), 2048)
            copies.append(
                pltpu.make_async_copy(out.at[:, part], out_h.at[:, part], sems.at[q // 8])
            )
            copies[-1].start()
    for copy in copies:
        copy.wait()


def downward(top, coupling, levels, quads, pairs, nears):
    return pl.pallas_call(
        functools.partial(down_kernel, len(nears)),
        out_shape=jax.ShapeDtypeStruct((64, 8192), F32),
        in_specs=[pl.BlockSpec(memory_space=VMEM)] * (5 + len(nears)),
        out_specs=pl.BlockSpec(memory_space=pl.ANY),
        scratch_shapes=[
            VMEM((64, 8064), F32),
            VMEM((31 * 64, 128), BF16),
            VMEM((64, 8192), F32),
            pltpu.SemaphoreType.DMA((4,)),
        ],
        compiler_params=pltpu.CompilerParams(vmem_limit_bytes=36 * 2**20),
        cost_estimate=pl.CostEstimate(flops=10**9, bytes_accessed=8 * 2**20, transcendentals=0),
        name="downward",
    )(top, coupling, levels, quads, pairs, *nears)


def exchanged(value, mask):
    devices = lax.axis_size(AXES)
    return lax.ppermute(value, AXES, [(s, s ^ mask) for s in range(devices)])


def dot(a, b):
    return jnp.dot(a, b, precision=HIGH)


def on_device(coords, vectors, bases, transfer, coupling, top_transfer, top_coupling):
    vectors = vectors.T
    device = lax.axis_index(AXES).astype(jnp.int32).reshape(1)
    climbing, levels, pairs, quads = upward(
        bases.transpose(1, 2, 0), vectors, transfer[0].transpose(1, 2, 0)
    )
    own, sib, lift = top_matrices(
        device, top_transfer.transpose(1, 2, 0), top_coupling.transpose(1, 2, 0)
    )
    nears = []
    top = jnp.zeros((64, 64), F32)
    for height in range(8):
        partner = exchanged(climbing, 1 << height)
        if 1 <= height <= 4:
            nears.append(near(coords, vectors, 8 * len(nears), 8))
        top = top + dot(partner, lift[height])
        if height < 7:
            climbing = dot(climbing, own[height]) + dot(partner, sib[height])
    result = downward(top, coupling[0], levels, quads, pairs, nears)
    return result.T


def solution(mesh):
    both = ("leaf", "sub")
    return jax.shard_map(
        on_device,
        mesh=mesh,
        in_specs=(
            P(None, both),
            P(both, None),
            P(both, None, None),
            P(both, None, None, None),
            P(both, None, None, None),
            P(),
            P(),
        ),
        out_specs=P(both, None),
        check_vma=False,
    )
```

```python
import functools

import jax
import jax.numpy as jnp
from jax import lax
from jax.experimental import pallas as pl
from jax.experimental.pallas import tpu as pltpu
from jax.sharding import PartitionSpec as P

F32 = jnp.float32
BF16 = jnp.bfloat16
VMEM = pltpu.VMEM
AXES = ("leaf", "sub")
HIGH = lax.Precision.HIGHEST

STEP = 136
NN = (((1,), (0,)), ((), ()))
NT = (((1,), (1,)), ((), ()))
LEVEL_AT = (None, 0, 4096, 6144, 7168, 7680, 7936)
NODE_AT = (0, 128, 192, 224, 240, 248, 252)
NUGGET_DIAG = 1.5
MASKS = (1, 2, 6, 8, 16, 48, 64, 192)
BESIDE = {4: (0,), 5: (1,), 6: (2,), 7: (3,)}
CHORD = 2.0 * 1.4426950408889634


def mxu(a, b, dims):
    return lax.dot_general(a, b, dims, preferred_element_type=F32)


def split(c):
    hi = c.astype(BF16)
    lo = (c - hi.astype(F32)).astype(BF16)
    return jnp.concatenate([hi, lo], 0)


def fold(t):
    half = t.shape[0] // 2
    return t[:half] + t[half:]


def half_mask():
    return lax.broadcasted_iota(jnp.int32, (32, 128), 1) < 64


def spread(src, width, lane0, slab, rows):
    for i in rows:
        w = jnp.concatenate([src[i, :, lane0 : lane0 + width], src[i + 32, :, lane0 : lane0 + width]], 0)
        if width < 128:
            w = jnp.concatenate([w, jnp.zeros((128, 128 - width), BF16)], 1)
        slab[pl.ds(i * STEP, 128), :] = w.T.astype(F32)


def box_matrix(slab, box, right, low):
    x = slab[pl.ds(box, 32, stride=STEP), :]
    y = pltpu.roll(x, 64, 1)
    if right:
        return jnp.concatenate([jnp.where(low, 0.0, y), jnp.where(low, 0.0, x)], 0)
    return jnp.concatenate([jnp.where(low, x, 0.0), jnp.where(low, y, 0.0)], 0)


def up_kernel(
    bases_h, vectors_h, transfer_h, own_out, levels_h, pairs_h, quads_h,
    bases, vectors, transfer, slab0, slab1, slab2, leaf_coef, levels, pairs, quads, sems, out_sems,
):
    loads = []
    for k in range(4):
        part = pl.ds(16 * (k // 2) + 32 * (k % 2), 16)
        loads.append(pltpu.make_async_copy(bases_h.at[part], bases.at[part], sems.at[k]))
    loads.append(pltpu.make_async_copy(vectors_h, vectors, sems.at[4]))
    loads.append(pltpu.make_async_copy(transfer_h, transfer, sems.at[5]))
    for copy in loads:
        copy.start()
    stores = []

    def store(src, dst):
        copy = pltpu.make_async_copy(src, dst, out_sems.at[len(stores)])
        copy.start()
        stores.append(copy)

    low = half_mask()
    for k in range(2):
        loads[2 * k].wait()
        loads[2 * k + 1].wait()
        spread(bases, 128, 0, slab0, range(16 * k, 16 * k + 16))
    loads[4].wait()
    for j in range(64):
        pair = jnp.concatenate(
            [box_matrix(slab0, 2 * j, False, low), box_matrix(slab0, 2 * j + 1, True, low)], 0
        ).astype(BF16)
        pairs[j] = pair
        leaf_coef[:, 128 * j : 128 * j + 128] = mxu(
            vectors[:, 128 * j : 128 * j + 128], pair, NN
        )
    store(pairs, pairs_h)
    loads[5].wait()
    spread(transfer, 128, 0, slab1, range(32))
    spread(transfer, 126, 128, slab2, range(32))
    for level in range(6):
        count = 128 >> level
        for q in range(count // 4):
            first = NODE_AT[level] + 4 * q
            slab = slab1 if first < 128 else slab2
            quad = jnp.concatenate(
                [box_matrix(slab, (first + u) % 128, u >= 2, low) for u in range(4)], 0
            ).astype(BF16)
            quads[first // 4] = quad
            if level == 0:
                coef = leaf_coef[:, 256 * q : 256 * q + 256]
            else:
                at = LEVEL_AT[level] + 256 * q
                coef = levels[:, at : at + 256]
            at = LEVEL_AT[level + 1] + 128 * q
            levels[:, at : at + 128] = fold(mxu(split(coef), quad, NN))
        if level < 2:
            part = pl.ds(NODE_AT[level] // 4, count // 4)
            store(quads.at[part], quads_h.at[part])
            part = pl.ds(LEVEL_AT[level + 1], 32 * count)
            store(levels.at[:, part], levels_h.at[:, part])
    last = jnp.concatenate(
        [box_matrix(slab2, 124, False, low), box_matrix(slab2, 125, False, low)], 0
    ).astype(BF16)
    quads[63, :128, :] = last
    quads[63, 128:, :] = jnp.zeros((128, 128), BF16)
    part = pl.ds(48, 16)
    store(quads.at[part], quads_h.at[part])
    part = pl.ds(LEVEL_AT[3], 1920)
    store(levels.at[:, part], levels_h.at[:, part])
    at = LEVEL_AT[6]
    own_out[...] = fold(mxu(split(levels[:, at : at + 128]), last, NN))[:, :64]
    for copy in stores:
        copy.wait()


def params(mib):
    return pltpu.CompilerParams(vmem_limit_bytes=mib * 2**20)


def cost(us):
    return pl.CostEstimate(flops=int(us * 10**9), bytes_accessed=2**16, transcendentals=0)


IN_VMEM = pl.BlockSpec(memory_space=VMEM)
IN_HBM = pl.BlockSpec(memory_space=pl.ANY)
IN_SMEM = pl.BlockSpec(memory_space=pltpu.SMEM)


def upward(bases, vectors, transfer):
    return pl.pallas_call(
        up_kernel,
        out_shape=[
            jax.ShapeDtypeStruct((64, 64), F32),
            jax.ShapeDtypeStruct((64, 8064), F32),
            jax.ShapeDtypeStruct((64, 128, 128), BF16),
            jax.ShapeDtypeStruct((64, 256, 128), BF16),
        ],
        in_specs=[IN_HBM] * 3,
        out_specs=[IN_VMEM] + [IN_HBM] * 3,
        scratch_shapes=[
            VMEM((64, 64, 128), BF16),
            VMEM((64, 8192), BF16),
            VMEM((64, 64, 254), BF16),
            VMEM((32 * STEP, 128), F32),
            VMEM((32 * STEP, 128), F32),
            VMEM((32 * STEP, 128), F32),
            VMEM((64, 8192), F32),
            VMEM((64, 8064), F32),
            VMEM((64, 128, 128), BF16),
            VMEM((64, 256, 128), BF16),
            pltpu.SemaphoreType.DMA((6,)),
            pltpu.SemaphoreType.DMA((7,)),
        ],
        compiler_params=params(58),
        cost_estimate=cost(8),
        name="upward",
    )(bases, vectors, transfer)


def pick_rows(table, pick, slab):
    for i in range(16):
        rows = jnp.concatenate(
            [table[2 * i], table[2 * i + 32], table[2 * i + 1], table[2 * i + 33]], 0
        )
        out = mxu(pick, rows, NT)
        slab[pl.ds(48 * i, 16), :] = out[:, :128]
        slab[pl.ds(48 * i + 24, 16), :] = out[:, 128:]


def picked(slab, row):
    x = slab[pl.ds(row, 32, stride=24), :]
    return jnp.concatenate([x, pltpu.roll(x, 64, 1)], 0)[:, :64]


def transfer_pick(dev, heights, lane0, width):
    row = lax.broadcasted_iota(jnp.int32, (16, width), 0)
    col = lax.broadcasted_iota(jnp.int32, (16, width), 1)
    hit = jnp.zeros((16, width), jnp.bool_)
    for n, height in enumerate(heights):
        box = 512 - (512 >> height) + (dev >> height) - lane0
        hit = hit | ((row == n) & (col == box))
        hit = hit | ((row == n + 8) & (col == (box ^ 1)))
    return jnp.where(hit, 1.0, 0.0).astype(BF16)


def thirds(x):
    a = x.astype(BF16).astype(F32)
    b = (x - a).astype(BF16).astype(F32)
    return a, b, x - a - b


def near_field(coords, vectors, out, square_x, left_t, right):
    square_x[0:3, :] = coords[...] * CHORD
    square_x[3:8, :] = jnp.zeros((5, 2048), F32)
    x = square_x[...]
    one8 = jnp.where(lax.broadcasted_iota(jnp.int32, (8, 2048), 0) == 0, 1.0, 0.0)
    x1, x2, x3 = thirds(x)
    n1, n2, n3 = thirds(jnp.sum(x * x, axis=0, keepdims=True) * one8)
    left = jnp.concatenate([x1, x1, x2, x2, x1, x3, n1, n2, n3, one8, one8, one8], 0)
    left_t[...] = left.astype(BF16).T
    y1, y2, y3 = -2 * x1, -2 * x2, -2 * x3
    right[...] = jnp.concatenate(
        [y1, y2, y1, y2, y3, y1, one8, one8, one8, n1, n2, n3], 0
    ).astype(BF16)
    eye = (
        lax.broadcasted_iota(jnp.int32, (128, 128), 0)
        == lax.broadcasted_iota(jnp.int32, (128, 128), 1)
    )
    for g in range(8):
        at = 256 * g

        def block(a, b):
            square = mxu(left_t[at + a : at + a + 128, :], right[:, at + b : at + b + 128], NN)
            square = jnp.maximum(square, 1e-30)
            value = jnp.exp2(-(square * lax.rsqrt(square)))
            if a == b:
                value = jnp.where(eye, NUGGET_DIAG, value)
            return value.astype(BF16)

        v0 = vectors[:, at : at + 128]
        v1 = vectors[:, at + 128 : at + 256]
        side = block(0, 128)
        out[:, at : at + 128] = mxu(v0, block(0, 0), NN) + mxu(v1, side, NT)
        out[:, at + 128 : at + 256] = mxu(v0, side, NN) + mxu(v1, block(128, 128), NN)


NEAR_SCRATCH = [
    VMEM((3, 2048), F32),
    VMEM((64, 2048), BF16),
    VMEM((8, 2048), F32),
    VMEM((2048, 96), BF16),
    VMEM((96, 2048), BF16),
]


def start_near(piece, coords_h, vectors_h, coords, vectors, sems):
    part = pl.ds(2048 * piece, 2048)
    copies = [
        pltpu.make_async_copy(coords_h.at[:, part], coords, sems.at[0]),
        pltpu.make_async_copy(vectors_h.at[:, part], vectors, sems.at[1]),
    ]
    for copy in copies:
        copy.start()
    return copies


def first_kernel(after, device, transfer_h, own_out, sib_out, table, slab, sems):
    dev = device[0]
    lane0 = pl.multiple_of(128 * (dev >> 7), 128)
    load = pltpu.make_async_copy(transfer_h.at[:, :, pl.ds(lane0, 128)], table, sems.at[0])
    load.start()
    load.wait()
    pick_rows(table, transfer_pick(dev, [0], lane0, 128), slab)
    own_out[...] = picked(slab, 0)
    sib_out[...] = picked(slab, 8)


def first_pick(after, device, transfer):
    return pl.pallas_call(
        first_kernel,
        out_shape=[jax.ShapeDtypeStruct((64, 64), F32)] * 2,
        in_specs=[IN_VMEM, IN_SMEM, IN_HBM],
        out_specs=[IN_VMEM] * 2,
        scratch_shapes=[
            VMEM((64, 64, 128), BF16),
            VMEM((32 * 24, 128), F32),
            pltpu.SemaphoreType.DMA((1,)),
        ],
        compiler_params=params(58),
        cost_estimate=cost(1),
        name="first_pick",
    )(after, device, transfer)


def second_kernel(
    after, device, coords_h, vectors_h, transfer_h, near_out, own_out, sib_out,
    coords, vectors, square_x, left_t, right, table, slab, sems,
):
    dev = device[0]
    load = pltpu.make_async_copy(transfer_h.at[:, :, pl.ds(256, 252)], table, sems.at[2])
    load.start()
    for copy in start_near(0, coords_h, vectors_h, coords, vectors, sems):
        copy.wait()
    near_field(coords, vectors, near_out, square_x, left_t, right)
    load.wait()
    pick_rows(table, transfer_pick(dev, range(1, 7), 256, 252), slab)
    for n in range(6):
        own_out[n] = picked(slab, n)
        sib_out[n] = picked(slab, 8 + n)


def second_pick(after, device, coords, vectors, transfer):
    return pl.pallas_call(
        second_kernel,
        out_shape=[jax.ShapeDtypeStruct((64, 2048), F32)]
        + [jax.ShapeDtypeStruct((6, 64, 64), F32)] * 2,
        in_specs=[IN_VMEM, IN_SMEM] + [IN_HBM] * 3,
        out_specs=[IN_VMEM] * 3,
        scratch_shapes=NEAR_SCRATCH
        + [
            VMEM((64, 64, 252), BF16),
            VMEM((32 * 24, 128), F32),
            pltpu.SemaphoreType.DMA((3,)),
        ],
        compiler_params=params(58),
        cost_estimate=cost(2),
        name="second_pick",
    )(after, device, coords, vectors, transfer)


def lift_kernel(
    after, device, own0, own, coords_h, vectors_h, coupling_h, near_out, lift_out,
    coords, vectors, square_x, left_t, right, table, slab, sems,
):
    dev = device[0]
    load = pltpu.make_async_copy(coupling_h, table, sems.at[2])
    load.start()
    for copy in start_near(1, coords_h, vectors_h, coords, vectors, sems):
        copy.wait()
    near_field(coords, vectors, near_out, square_x, left_t, right)
    load.wait()
    row = lax.broadcasted_iota(jnp.int32, (16, 255), 0)
    col = lax.broadcasted_iota(jnp.int32, (16, 255), 1)
    want = 256 - (256 >> row) + (jnp.full_like(row, dev) >> (row + 1))
    pick_rows(table, jnp.where((col == want) & (row < 8), 1.0, 0.0).astype(BF16), slab)
    chain = None
    for level in range(8):
        pair = picked(slab, level)
        odd = (dev >> level) & 1
        turned = jnp.where(odd == 1, pair, pair.T).astype(BF16)
        if level == 0:
            lift_out[0] = turned.astype(F32)
        else:
            hi = chain.astype(BF16)
            lo = (chain - hi.astype(F32)).astype(BF16)
            lift_out[level] = mxu(turned, hi, NN) + mxu(turned, lo, NN)
        if level < 7:
            e = (own0[...] if level == 0 else own[level - 1]).T
            if level == 0:
                chain = e
            else:
                e = e.astype(BF16)
                chain = mxu(e, hi, NN) + mxu(e, lo, NN)


def lifts(after, device, own0, own, coords, vectors, coupling):
    return pl.pallas_call(
        lift_kernel,
        out_shape=[
            jax.ShapeDtypeStruct((64, 2048), F32),
            jax.ShapeDtypeStruct((8, 64, 64), F32),
        ],
        in_specs=[IN_VMEM, IN_SMEM, IN_VMEM, IN_VMEM] + [IN_HBM] * 3,
        out_specs=[IN_VMEM] * 2,
        scratch_shapes=NEAR_SCRATCH
        + [
            VMEM((64, 64, 255), BF16),
            VMEM((32 * 24, 128), F32),
            pltpu.SemaphoreType.DMA((3,)),
        ],
        compiler_params=params(58),
        cost_estimate=cost(2),
        name="lifts",
    )(after, device, own0, own, coords, vectors, coupling)


def near_kernel(piece, after, coords_h, vectors_h, near_out, coords, vectors, square_x, left_t, right, sems):
    for copy in start_near(piece, coords_h, vectors_h, coords, vectors, sems):
        copy.wait()
    near_field(coords, vectors, near_out, square_x, left_t, right)


def near(piece, after, coords, vectors):
    return pl.pallas_call(
        functools.partial(near_kernel, piece),
        out_shape=jax.ShapeDtypeStruct((64, 2048), F32),
        in_specs=[IN_VMEM] + [IN_HBM] * 2,
        out_specs=IN_VMEM,
        scratch_shapes=NEAR_SCRATCH + [pltpu.SemaphoreType.DMA((2,))],
        compiler_params=params(58),
        cost_estimate=cost(1.5),
        name="near",
    )(after, coords, vectors)


def shift_right():
    row = lax.broadcasted_iota(jnp.int32, (64, 128), 0)
    col = lax.broadcasted_iota(jnp.int32, (64, 128), 1)
    return jnp.where(col == row + 64, 1.0, 0.0).astype(BF16)


def pair_field(coef, coupling, shift):
    z = mxu(coupling, shift, NN).astype(BF16)
    z = jnp.concatenate([z, jnp.zeros((64, 128), BF16)], 0)
    s = split(coef)
    return fold(mxu(s, z, NN) + mxu(s, z, NT))


def with_fields(state, fields):
    return jnp.concatenate([state[:64] + jnp.concatenate(fields, 1), state[64:]], 0)


def descend(state, quad):
    return fold(mxu(split(state), quad, NT))


def upper_kernel(after, coupling_h, levels_h, quads_h, state_out, coupling, levels, quads, sems):
    copies = [
        pltpu.make_async_copy(coupling_h.at[pl.ds(16, 15)], coupling, sems.at[0]),
        pltpu.make_async_copy(levels_h.at[:, pl.ds(LEVEL_AT[3], 1920)], levels, sems.at[1]),
        pltpu.make_async_copy(quads_h.at[pl.ds(56, 8)], quads, sems.at[2]),
    ]
    for copy in copies:
        copy.start()
    for copy in copies:
        copy.wait()
    shift = shift_right()

    def field(level, pair):
        base = 16 - (32 >> (level - 2))
        at = LEVEL_AT[level] - LEVEL_AT[3] + 128 * pair
        return pair_field(levels[:, at : at + 128], coupling[base + pair], shift)

    unit = jnp.where(
        lax.broadcasted_iota(jnp.int32, (64, 64), 0)
        == lax.broadcasted_iota(jnp.int32, (64, 64), 1),
        1.0,
        0.0,
    ).astype(BF16)
    state = jnp.concatenate([field(6, 0), mxu(unit, quads[7, :128, :64], NT)], 0)
    for level in range(5, 2, -1):
        below = []
        for q in range((128 >> level) // 4):
            s = descend(state[:, 128 * q : 128 * q + 128], quads[NODE_AT[level] // 4 - 56 + q])
            below.append(with_fields(s, [field(level, 2 * q), field(level, 2 * q + 1)]))
        state = jnp.concatenate(below, 1)
    state_out[...] = state


def upper(after, coupling, levels, quads):
    return pl.pallas_call(
        upper_kernel,
        out_shape=jax.ShapeDtypeStruct((128, 1024), F32),
        in_specs=[IN_VMEM] + [IN_HBM] * 3,
        out_specs=IN_VMEM,
        scratch_shapes=[
            VMEM((15, 64, 64), BF16),
            VMEM((64, 1920), F32),
            VMEM((8, 256, 128), BF16),
            pltpu.SemaphoreType.DMA((3,)),
        ],
        compiler_params=params(58),
        cost_estimate=cost(1.5),
        name="upper",
    )(after, coupling, levels, quads)


def lower_kernel(
    piece, after, state3, near_in, coupling_h, levels_h, quads_h, pairs_h, base_out, top_out,
    coupling, levels, quads, pairs, sems,
):
    copies = [
        pltpu.make_async_copy(coupling_h.at[pl.ds(4 * piece, 4)], coupling, sems.at[0]),
        pltpu.make_async_copy(
            levels_h.at[:, pl.ds(LEVEL_AT[2] + 512 * piece, 512)], levels, sems.at[1]
        ),
        pltpu.make_async_copy(quads_h.at[pl.ds(48 + 2 * piece, 2)], quads.at[pl.ds(12, 2)], sems.at[2]),
        pltpu.make_async_copy(quads_h.at[pl.ds(32 + 4 * piece, 4)], quads.at[pl.ds(8, 4)], sems.at[3]),
        pltpu.make_async_copy(quads_h.at[pl.ds(8 * piece, 8)], quads.at[pl.ds(0, 8)], sems.at[4]),
        pltpu.make_async_copy(pairs_h.at[pl.ds(16 * piece, 16)], pairs, sems.at[5]),
    ]
    for copy in copies:
        copy.start()
    shift = shift_right()
    copies[0].wait()
    copies[1].wait()
    fields = [
        pair_field(levels[:, 128 * p : 128 * p + 128], coupling[p], shift) for p in range(4)
    ]
    for copy in copies[2:]:
        copy.wait()
    state = state3[:, 256 * piece : 256 * piece + 256]
    state = jnp.concatenate(
        [
            with_fields(
                descend(state[:, 128 * q : 128 * q + 128], quads[12 + q]),
                fields[2 * q : 2 * q + 2],
            )
            for q in range(2)
        ],
        1,
    )
    state = jnp.concatenate(
        [descend(state[:, 128 * q : 128 * q + 128], quads[8 + q]) for q in range(4)], 1
    )
    for q in range(8):
        leaf = descend(state[:, 128 * q : 128 * q + 128], quads[q])
        for u in range(2):
            at = 256 * q + 128 * u
            t = descend(leaf[:, 128 * u : 128 * u + 128], pairs[2 * q + u])
            base_out[:, at : at + 128] = t[:64] + near_in[:, at : at + 128]
            top_out[:, at : at + 128] = split(t[64:])


def lower_piece(piece, after, state3, near_in, coupling, levels, quads, pairs):
    return pl.pallas_call(
        functools.partial(lower_kernel, piece),
        out_shape=[
            jax.ShapeDtypeStruct((64, 2048), F32),
            jax.ShapeDtypeStruct((128, 2048), BF16),
        ],
        in_specs=[IN_VMEM] * 3 + [IN_HBM] * 4,
        out_specs=[IN_VMEM] * 2,
        scratch_shapes=[
            VMEM((4, 64, 64), BF16),
            VMEM((64, 512), F32),
            VMEM((14, 256, 128), BF16),
            VMEM((16, 128, 128), BF16),
            pltpu.SemaphoreType.DMA((6,)),
        ],
        compiler_params=params(50),
        cost_estimate=cost(1.5),
        name="lower",
    )(after, state3, near_in, coupling, levels, quads, pairs)


def final_kernel(lift, *refs):
    partners = refs[:8]
    bases = refs[8:12]
    tops = refs[12:16]
    out_h, out, sems = refs[16:]
    g = jnp.zeros((64, 64), F32)
    for height in range(8):
        w = lift[height]
        hi = w.astype(BF16)
        lo = (w - hi.astype(F32)).astype(BF16)
        p = split(partners[height][...])
        g = g + fold(mxu(p, hi, NN)) + mxu(p[:64], lo, NN)
    hi = g.astype(BF16)
    lo = (g - hi.astype(F32)).astype(BF16)
    g = jnp.concatenate(
        [jnp.concatenate([hi, hi], 1), jnp.concatenate([lo, jnp.zeros_like(lo)], 1)], 0
    )
    copies = []
    for piece in range(4):
        for q in range(8):
            at = 256 * q
            out[:, 2048 * piece + at : 2048 * piece + at + 256] = (
                fold(mxu(g, tops[piece][:, at : at + 256], NN)) + bases[piece][:, at : at + 256]
            )
        part = pl.ds(2048 * piece, 2048)
        copies.append(pltpu.make_async_copy(out.at[:, part], out_h.at[:, part], sems.at[piece]))
        copies[-1].start()
    for copy in copies:
        copy.wait()


def final(lift, partners, bases, tops):
    return pl.pallas_call(
        final_kernel,
        out_shape=jax.ShapeDtypeStruct((64, 8192), F32),
        in_specs=[IN_VMEM] * 17,
        out_specs=IN_HBM,
        scratch_shapes=[VMEM((64, 8192), F32), pltpu.SemaphoreType.DMA((4,))],
        compiler_params=params(16),
        cost_estimate=cost(2),
        name="final",
    )(lift, *partners, *bases, *tops)


def exchanged(value, mask):
    devices = lax.axis_size(AXES)
    return lax.ppermute(value, AXES, [(s, s ^ mask) for s in range(devices)])


def dot(a, b):
    return jnp.dot(a, b, precision=HIGH)


def on_device(coords, vectors, bases, transfer, coupling, top_transfer, top_coupling):
    vectors = vectors.T
    device = lax.axis_index(AXES).astype(jnp.int32).reshape(1)
    climbing, levels, pairs, quads = upward(
        bases.transpose(1, 2, 0), vectors, transfer[0].transpose(1, 2, 0)
    )
    top_transfer = top_transfer.transpose(1, 2, 0)
    top_coupling = top_coupling.transpose(1, 2, 0)
    coupling = coupling[0]
    partners, nears, lows = [], [None] * 4, []
    for height, mask in enumerate(MASKS):
        partner = exchanged(climbing, mask)
        if height == 0:
            own0, sib0 = first_pick(climbing, device, top_transfer)
            own, sib = [own0], [sib0]
        elif height == 1:
            nears[0], owns, sibs = second_pick(climbing, device, coords, vectors, top_transfer)
            own += [owns[n] for n in range(6)]
            sib += [sibs[n] for n in range(6)]
        elif height == 2:
            nears[1], lift = lifts(climbing, device, own0, owns, coords, vectors, top_coupling)
        elif height == 3:
            nears[2] = near(2, climbing, coords, vectors)
            state = upper(climbing, coupling, levels, quads)
        elif height == 4:
            nears[3] = near(3, climbing, coords, vectors)
        for piece in BESIDE.get(height, ()):
            lows.append(
                lower_piece(piece, climbing, state, nears[piece], coupling, levels, quads, pairs)
            )
        partners.append(partner)
        if height < 7:
            climbing = dot(climbing, own[height]) + dot(partner, sib[height])
    result = final(lift, partners, [low[0] for low in lows], [low[1] for low in lows])
    return result.T


def solution(mesh):
    both = ("leaf", "sub")
    return jax.shard_map(
        on_device,
        mesh=mesh,
        in_specs=(
            P(None, both),
            P(both, None),
            P(both, None, None),
            P(both, None, None, None),
            P(both, None, None, None),
            P(),
            P(),
        ),
        out_specs=P(both, None),
        check_vma=False,
    )
```

```python
import functools

import jax
import jax.numpy as jnp
from jax import lax
from jax.experimental import pallas as pl
from jax.experimental.pallas import tpu as pltpu
from jax.sharding import PartitionSpec as P

F32 = jnp.float32
BF16 = jnp.bfloat16
VMEM = pltpu.VMEM
AXES = ("leaf", "sub")
HIGH = lax.Precision.HIGHEST

STEP = 136
NN = (((1,), (0,)), ((), ()))
NT = (((1,), (1,)), ((), ()))
LEVEL_AT = (None, 0, 4096, 6144, 7168, 7680, 7936)
NODE_AT = (0, 128, 192, 224, 240, 248, 252)
NUGGET_DIAG = 1.5
MASKS = (1, 2, 6, 8, 16, 48, 64, 192)
NEAR_BESIDE = {2: (0, 1), 3: (2,), 5: (3,)}
BESIDE = {5: (0,), 6: (1, 2), 7: (3,)}
CHORD = 2.0 * 1.4426950408889634


def mxu(a, b, dims):
    return lax.dot_general(a, b, dims, preferred_element_type=F32)


def split(c):
    hi = c.astype(BF16)
    lo = (c - hi.astype(F32)).astype(BF16)
    return jnp.concatenate([hi, lo], 0)


def fold(t):
    half = t.shape[0] // 2
    return t[:half] + t[half:]


def half_mask():
    return lax.broadcasted_iota(jnp.int32, (32, 128), 1) < 64


def spread(src, width, lane0, slab, rows):
    for i in rows:
        w = jnp.concatenate([src[i, :, lane0 : lane0 + width], src[i + 32, :, lane0 : lane0 + width]], 0)
        if width < 128:
            w = jnp.concatenate([w, jnp.zeros((128, 128 - width), BF16)], 1)
        slab[pl.ds(i * STEP, 128), :] = w.T.astype(F32)


def box_matrix(slab, box, right, low):
    x = slab[pl.ds(box, 32, stride=STEP), :]
    y = pltpu.roll(x, 64, 1)
    if right:
        return jnp.concatenate([jnp.where(low, 0.0, y), jnp.where(low, 0.0, x)], 0)
    return jnp.concatenate([jnp.where(low, x, 0.0), jnp.where(low, y, 0.0)], 0)


def up_kernel(
    device, bases_h, vectors_h, transfer_h, top_transfer_h, top_coupling_h,
    own_out, table0, table1, table2, levels_h, pairs_h, quads_h,
    bases, vectors, transfer, slab0, slab1, slab2, leaf_coef, levels, pairs, quads, sems, out_sems,
):
    loads = []
    for k in range(4):
        part = pl.ds(16 * (k // 2) + 32 * (k % 2), 16)
        loads.append(pltpu.make_async_copy(bases_h.at[part], bases.at[part], sems.at[k]))
    loads.append(pltpu.make_async_copy(vectors_h, vectors, sems.at[4]))
    loads.append(pltpu.make_async_copy(transfer_h, transfer, sems.at[5]))
    lane0 = pl.multiple_of(128 * (device[0] >> 7), 128)
    tables = [
        (top_transfer_h.at[:, :, pl.ds(lane0, 128)], table0),
        (top_transfer_h.at[:, :, pl.ds(256, 252)], table1),
        (top_coupling_h, table2),
    ]
    loads += [
        pltpu.make_async_copy(src, dst, sems.at[6 + n]) for n, (src, dst) in enumerate(tables)
    ]
    for copy in loads:
        copy.start()
    stores = []

    def store(src, dst):
        copy = pltpu.make_async_copy(src, dst, out_sems.at[len(stores)])
        copy.start()
        stores.append(copy)

    low = half_mask()
    for k in range(2):
        loads[2 * k].wait()
        loads[2 * k + 1].wait()
        spread(bases, 128, 0, slab0, range(16 * k, 16 * k + 16))
    loads[4].wait()
    held = []
    for j in range(64 + DEPTH):
        if j == 16:
            loads[5].wait()
        if j < 64:
            pair = jnp.concatenate(
                [box_matrix(slab0, 2 * j, False, low), box_matrix(slab0, 2 * j + 1, True, low)], 0
            ).astype(BF16)
            pairs[j] = pair
            held.append(pair)
        if 16 <= j < 48:
            spread(transfer, 128, 0, slab1, [j - 16])
        if j >= DEPTH:
            at = 128 * (j - DEPTH)
            leaf_coef[:, at : at + 128] = mxu(vectors[:, at : at + 128], held[j - DEPTH], NN)
    store(pairs, pairs_h)
    steps = [(level, q) for level in range(6) for q in range((128 >> level) // 4)]
    held = []
    for k in range(len(steps) + UP_DEPTH):
        if k < 16:
            spread(transfer, 126, 128, slab2, [2 * k, 2 * k + 1])
        if k < len(steps):
            level, q = steps[k]
            first = NODE_AT[level] + 4 * q
            slab = slab1 if first < 128 else slab2
            quad = jnp.concatenate(
                [box_matrix(slab, (first + u) % 128, u >= 2, low) for u in range(4)], 0
            ).astype(BF16)
            quads[first // 4] = quad
            held.append(quad)
        if k >= UP_DEPTH:
            level, q = steps[k - UP_DEPTH]
            count = 128 >> level
            if level == 0:
                coef = leaf_coef[:, 256 * q : 256 * q + 256]
            else:
                at = LEVEL_AT[level] + 256 * q
                coef = levels[:, at : at + 256]
            at = LEVEL_AT[level + 1] + 128 * q
            levels[:, at : at + 128] = fold(mxu(split(coef), held[k - UP_DEPTH], NN))
            if level < 2 and q == count // 4 - 1:
                part = pl.ds(NODE_AT[level] // 4, count // 4)
                store(quads.at[part], quads_h.at[part])
                part = pl.ds(LEVEL_AT[level + 1], 32 * count)
                store(levels.at[:, part], levels_h.at[:, part])
    last = jnp.concatenate(
        [box_matrix(slab2, 124, False, low), box_matrix(slab2, 125, False, low)], 0
    ).astype(BF16)
    quads[63, :128, :] = last
    quads[63, 128:, :] = jnp.zeros((128, 128), BF16)
    part = pl.ds(48, 16)
    store(quads.at[part], quads_h.at[part])
    part = pl.ds(LEVEL_AT[3], 1920)
    store(levels.at[:, part], levels_h.at[:, part])
    at = LEVEL_AT[6]
    own_out[...] = fold(mxu(split(levels[:, at : at + 128]), last, NN))[:, :64]
    for copy in loads[6:] + stores:
        copy.wait()


def params(mib):
    return pltpu.CompilerParams(vmem_limit_bytes=mib * 2**20)


def cost(us):
    return pl.CostEstimate(flops=int(us * 10**9), bytes_accessed=2**16, transcendentals=0)


UP_MIB = 52
WINDOW_MIB = 12
UP_DEPTH = 4
DEPTH = 2
IN_VMEM = pl.BlockSpec(memory_space=VMEM)
IN_HBM = pl.BlockSpec(memory_space=pl.ANY)
IN_SMEM = pl.BlockSpec(memory_space=pltpu.SMEM)


def upward(device, bases, vectors, transfer, top_transfer, top_coupling):
    return pl.pallas_call(
        up_kernel,
        out_shape=[
            jax.ShapeDtypeStruct((64, 64), F32),
            jax.ShapeDtypeStruct((64, 64, 128), BF16),
            jax.ShapeDtypeStruct((64, 64, 252), BF16),
            jax.ShapeDtypeStruct((64, 64, 255), BF16),
            jax.ShapeDtypeStruct((64, 8064), F32),
            jax.ShapeDtypeStruct((64, 128, 128), BF16),
            jax.ShapeDtypeStruct((64, 256, 128), BF16),
        ],
        in_specs=[IN_SMEM] + [IN_HBM] * 5,
        out_specs=[IN_VMEM] * 4 + [IN_HBM] * 3,
        scratch_shapes=[
            VMEM((64, 64, 128), BF16),
            VMEM((64, 8192), BF16),
            VMEM((64, 64, 254), BF16),
            VMEM((32 * STEP, 128), F32),
            VMEM((32 * STEP, 128), F32),
            VMEM((32 * STEP, 128), F32),
            VMEM((64, 8192), F32),
            VMEM((64, 8064), F32),
            VMEM((64, 128, 128), BF16),
            VMEM((64, 256, 128), BF16),
            pltpu.SemaphoreType.DMA((9,)),
            pltpu.SemaphoreType.DMA((7,)),
        ],
        compiler_params=params(UP_MIB),
        cost_estimate=cost(8),
        name="upward",
    )(device, bases, vectors, transfer, top_transfer, top_coupling)


def pick_rows(table, pick, slab):
    for i in range(16):
        rows = jnp.concatenate(
            [table[2 * i], table[2 * i + 32], table[2 * i + 1], table[2 * i + 33]], 0
        )
        out = mxu(pick, rows, NT)
        slab[pl.ds(48 * i, 16), :] = out[:, :128]
        slab[pl.ds(48 * i + 24, 16), :] = out[:, 128:]


def picked(slab, row):
    x = slab[pl.ds(row, 32, stride=24), :]
    return jnp.concatenate([x, pltpu.roll(x, 64, 1)], 0)[:, :64]


def transfer_pick(dev, heights, lane0, width):
    row = lax.broadcasted_iota(jnp.int32, (16, width), 0)
    col = lax.broadcasted_iota(jnp.int32, (16, width), 1)
    hit = jnp.zeros((16, width), jnp.bool_)
    for n, height in enumerate(heights):
        box = 512 - (512 >> height) + (dev >> height) - lane0
        hit = hit | ((row == n) & (col == box))
        hit = hit | ((row == n + 8) & (col == (box ^ 1)))
    return jnp.where(hit, 1.0, 0.0).astype(BF16)


def thirds(x):
    a = x.astype(BF16).astype(F32)
    b = (x - a).astype(BF16).astype(F32)
    return a, b, x - a - b


def near_field(piece, coords, vectors, out, square_x, left_t, right):
    square_x[0:3, :] = coords[:, 2048 * piece : 2048 * piece + 2048] * CHORD
    square_x[3:8, :] = jnp.zeros((5, 2048), F32)
    x = square_x[...]
    one8 = jnp.where(lax.broadcasted_iota(jnp.int32, (8, 2048), 0) == 0, 1.0, 0.0)
    x1, x2, x3 = thirds(x)
    n1, n2, n3 = thirds(jnp.sum(x * x, axis=0, keepdims=True) * one8)
    left = jnp.concatenate([x1, x1, x2, x2, x1, x3, n1, n2, n3, one8, one8, one8], 0)
    left_t[...] = left.astype(BF16).T
    y1, y2, y3 = -2 * x1, -2 * x2, -2 * x3
    right[...] = jnp.concatenate(
        [y1, y2, y1, y2, y3, y1, one8, one8, one8, n1, n2, n3], 0
    ).astype(BF16)
    eye = (
        lax.broadcasted_iota(jnp.int32, (128, 128), 0)
        == lax.broadcasted_iota(jnp.int32, (128, 128), 1)
    )
    held = []

    def apply(at, side, first, second):
        here = 2048 * piece + at
        v0 = vectors[:, here : here + 128]
        v1 = vectors[:, here + 128 : here + 256]
        out[:, at : at + 128] = mxu(v0, first, NN) + mxu(v1, side, NT)
        out[:, at + 128 : at + 256] = mxu(v0, side, NN) + mxu(v1, second, NN)

    for g in range(8 + DEPTH):
        if g < 8:
            at = 256 * g

            def block(a, b):
                square = mxu(left_t[at + a : at + a + 128, :], right[:, at + b : at + b + 128], NN)
                square = jnp.maximum(square, 1e-30)
                value = jnp.exp2(-(square * lax.rsqrt(square)))
                if a == b:
                    value = jnp.where(eye, NUGGET_DIAG, value)
                return value.astype(BF16)

            held.append((at, block(0, 128), block(0, 0), block(128, 128)))
        if g >= DEPTH:
            apply(*held[g - DEPTH])


NEAR_SCRATCH = [
    VMEM((8, 2048), F32),
    VMEM((2048, 96), BF16),
    VMEM((96, 2048), BF16),
]


def first_kernel(after, device, transfer, own_out, sib_out, slab):
    dev = device[0]
    lane0 = pl.multiple_of(128 * (dev >> 7), 128)
    pick_rows(transfer, transfer_pick(dev, [0], lane0, 128), slab)
    own_out[...] = picked(slab, 0)
    sib_out[...] = picked(slab, 8)


def first_pick(after, device, transfer):
    return pl.pallas_call(
        first_kernel,
        out_shape=[jax.ShapeDtypeStruct((64, 64), F32)] * 2,
        in_specs=[IN_VMEM, IN_SMEM, IN_VMEM],
        out_specs=[IN_VMEM] * 2,
        scratch_shapes=[VMEM((32 * 24, 128), F32)],
        compiler_params=params(WINDOW_MIB),
        cost_estimate=cost(1),
        name="first_pick",
    )(after, device, transfer)


def second_kernel(after, device, transfer, own_out, sib_out, slab):
    dev = device[0]
    pick_rows(transfer, transfer_pick(dev, range(1, 7), 256, 252), slab)
    for n in range(6):
        own_out[n] = picked(slab, n)
        sib_out[n] = picked(slab, 8 + n)


def second_pick(after, device, transfer):
    return pl.pallas_call(
        second_kernel,
        out_shape=[jax.ShapeDtypeStruct((6, 64, 64), F32)] * 2,
        in_specs=[IN_VMEM, IN_SMEM, IN_VMEM],
        out_specs=[IN_VMEM] * 2,
        scratch_shapes=[VMEM((32 * 24, 128), F32)],
        compiler_params=params(WINDOW_MIB),
        cost_estimate=cost(1),
        name="second_pick",
    )(after, device, transfer)


def lift_kernel(after, device, own0, own, table, lift_out, slab):
    dev = device[0]
    row = lax.broadcasted_iota(jnp.int32, (16, 255), 0)
    col = lax.broadcasted_iota(jnp.int32, (16, 255), 1)
    want = 256 - (256 >> row) + (jnp.full_like(row, dev) >> (row + 1))
    pick_rows(table, jnp.where((col == want) & (row < 8), 1.0, 0.0).astype(BF16), slab)
    turned = []
    for level in range(8):
        pair = picked(slab, level)
        odd = (dev >> level) & 1
        turned.append(jnp.where(odd == 1, pair, pair.T).astype(BF16))
    steps = [own0[...].T] + [own[n].T.astype(BF16) for n in range(6)]
    lift_out[0] = turned[0].astype(F32)
    chain = steps[0]
    for level in range(1, 8):
        hi = chain.astype(BF16)
        lo = (chain - hi.astype(F32)).astype(BF16)
        if level < 7:
            chain = mxu(steps[level], hi, NN) + mxu(steps[level], lo, NN)
        lift_out[level] = mxu(turned[level], hi, NN) + mxu(turned[level], lo, NN)


def lifts(after, device, own0, own, coupling):
    return pl.pallas_call(
        lift_kernel,
        out_shape=jax.ShapeDtypeStruct((8, 64, 64), F32),
        in_specs=[IN_VMEM, IN_SMEM, IN_VMEM, IN_VMEM, IN_VMEM],
        out_specs=IN_VMEM,
        scratch_shapes=[VMEM((32 * 24, 128), F32)],
        compiler_params=params(WINDOW_MIB),
        cost_estimate=cost(2),
        name="lifts",
    )(after, device, own0, own, coupling)


def near_kernel(piece, after, coords, vectors, near_out, square_x, left_t, right):
    near_field(piece, coords, vectors, near_out, square_x, left_t, right)


def near(piece, after, coords, vectors):
    return pl.pallas_call(
        functools.partial(near_kernel, piece),
        out_shape=jax.ShapeDtypeStruct((64, 2048), F32),
        in_specs=[IN_VMEM] * 3,
        out_specs=IN_VMEM,
        scratch_shapes=NEAR_SCRATCH,
        compiler_params=params(WINDOW_MIB),
        cost_estimate=cost(1.5),
        name="near",
    )(after, coords, vectors)


def shift_right():
    row = lax.broadcasted_iota(jnp.int32, (64, 128), 0)
    col = lax.broadcasted_iota(jnp.int32, (64, 128), 1)
    return jnp.where(col == row + 64, 1.0, 0.0).astype(BF16)


def pair_fields(coefs, couplings, shift):
    blank = jnp.zeros((64, 128), BF16)
    sides = [jnp.concatenate([mxu(c[...], shift, NN).astype(BF16), blank], 0) for c in couplings]
    parts = [split(c[...]) for c in coefs]
    terms = [(mxu(s, z, NN), mxu(s, z, NT)) for s, z in zip(parts, sides)]
    return [fold(a + b) for a, b in terms]


def with_fields(state, fields):
    return jnp.concatenate([state[:64] + jnp.concatenate(fields, 1), state[64:]], 0)


def descend(state, quad):
    return fold(mxu(split(state), quad, NT))


def upper_kernel(after, coupling, levels, quads, state_out):
    shift = shift_right()

    where = [(level, pair) for level in range(6, 2, -1) for pair in range((64 >> level))]
    found = pair_fields(
        [levels.at[:, pl.ds(LEVEL_AT[level] + 128 * pair, 128)] for level, pair in where],
        [coupling.at[32 - (32 >> (level - 2)) + pair] for level, pair in where],
        shift,
    )
    found = dict(zip(where, found))

    def field(level, pair):
        return found[level, pair]

    unit = jnp.where(
        lax.broadcasted_iota(jnp.int32, (64, 64), 0)
        == lax.broadcasted_iota(jnp.int32, (64, 64), 1),
        1.0,
        0.0,
    ).astype(BF16)
    state = jnp.concatenate([field(6, 0), mxu(unit, quads[63, :128, :64], NT)], 0)
    for level in range(5, 2, -1):
        below = []
        for q in range((128 >> level) // 4):
            s = descend(state[:, 128 * q : 128 * q + 128], quads[NODE_AT[level] // 4 + q])
            below.append(with_fields(s, [field(level, 2 * q), field(level, 2 * q + 1)]))
        state = jnp.concatenate(below, 1)
    state_out[...] = state


def upper(after, coupling, levels, quads):
    return pl.pallas_call(
        upper_kernel,
        out_shape=jax.ShapeDtypeStruct((128, 1024), F32),
        in_specs=[IN_VMEM] * 4,
        out_specs=IN_VMEM,
        compiler_params=params(WINDOW_MIB),
        cost_estimate=cost(1.5),
        name="upper",
    )(after, coupling, levels, quads)


def lower_kernel(piece, after, state3, near_in, coupling, levels, quads, pairs, base_out, top_out):
    shift = shift_right()
    mine = range(4 * piece, 4 * piece + 4)
    fields = pair_fields(
        [levels.at[:, pl.ds(LEVEL_AT[2] + 128 * p, 128)] for p in mine],
        [coupling.at[p] for p in mine],
        shift,
    )
    state = state3[:, 256 * piece : 256 * piece + 256]
    state = jnp.concatenate(
        [
            with_fields(
                descend(state[:, 128 * q : 128 * q + 128], quads[48 + 2 * piece + q]),
                fields[2 * q : 2 * q + 2],
            )
            for q in range(2)
        ],
        1,
    )
    state = jnp.concatenate(
        [descend(state[:, 128 * q : 128 * q + 128], quads[32 + 4 * piece + q]) for q in range(4)], 1
    )
    leaves = []
    for q in range(8 + DEPTH):
        if q < 8:
            leaves.append(descend(state[:, 128 * q : 128 * q + 128], quads[8 * piece + q]))
        if q >= DEPTH:
            for u in range(2):
                pair = 2 * (q - DEPTH) + u
                at = 128 * pair
                t = descend(
                    leaves[q - DEPTH][:, 128 * u : 128 * u + 128], pairs[16 * piece + pair]
                )
                base_out[:, at : at + 128] = t[:64] + near_in[:, at : at + 128]
                top_out[:, at : at + 128] = split(t[64:])


def lower_piece(piece, after, state3, near_in, coupling, levels, quads, pairs):
    return pl.pallas_call(
        functools.partial(lower_kernel, piece),
        out_shape=[
            jax.ShapeDtypeStruct((64, 2048), F32),
            jax.ShapeDtypeStruct((128, 2048), BF16),
        ],
        in_specs=[IN_VMEM] * 7,
        out_specs=[IN_VMEM] * 2,
        compiler_params=params(WINDOW_MIB),
        cost_estimate=cost(1.5),
        name="lower",
    )(after, state3, near_in, coupling, levels, quads, pairs)


def field_term(partner, lift):
    hi = lift.astype(BF16)
    lo = (lift - hi.astype(F32)).astype(BF16)
    p = split(partner)
    return fold(mxu(p, hi, NN)) + mxu(p[:64], lo, NN)


def partial_kernel(after, lift, *refs):
    terms = [field_term(refs[height][...], lift[height]) for height in range(7)]
    refs[7][...] = sum(terms[1:], terms[0])


def partial_field(after, lift, partners):
    return pl.pallas_call(
        partial_kernel,
        out_shape=jax.ShapeDtypeStruct((64, 64), F32),
        in_specs=[IN_VMEM] * 9,
        out_specs=IN_VMEM,
        compiler_params=params(WINDOW_MIB),
        cost_estimate=cost(0.5),
        name="partial_field",
    )(after, lift, *partners)


def final_kernel(lift, partial, partner, *refs):
    bases = refs[:4]
    tops = refs[4:8]
    out_h, out, sems = refs[8:]
    g = partial[...] + field_term(partner[...], lift[7])
    hi = g.astype(BF16)
    lo = (g - hi.astype(F32)).astype(BF16)
    g = jnp.concatenate(
        [jnp.concatenate([hi, hi], 1), jnp.concatenate([lo, jnp.zeros_like(lo)], 1)], 0
    )
    copies = []
    for piece in range(4):
        for q in range(8):
            at = 256 * q
            out[:, 2048 * piece + at : 2048 * piece + at + 256] = (
                fold(mxu(g, tops[piece][:, at : at + 256], NN)) + bases[piece][:, at : at + 256]
            )
        part = pl.ds(2048 * piece, 2048)
        copies.append(pltpu.make_async_copy(out.at[:, part], out_h.at[:, part], sems.at[piece]))
        copies[-1].start()
    for copy in copies:
        copy.wait()


def final(lift, partial, partner, bases, tops):
    return pl.pallas_call(
        final_kernel,
        out_shape=jax.ShapeDtypeStruct((64, 8192), F32),
        in_specs=[IN_VMEM] * 11,
        out_specs=IN_HBM,
        scratch_shapes=[VMEM((64, 8192), F32), pltpu.SemaphoreType.DMA((4,))],
        compiler_params=params(16),
        cost_estimate=cost(2),
        name="final",
    )(lift, partial, partner, *bases, *tops)


def exchanged(value, mask):
    devices = lax.axis_size(AXES)
    return lax.ppermute(value, AXES, [(s, s ^ mask) for s in range(devices)])


def dot(a, b):
    return jnp.dot(a, b, precision=HIGH)


def on_device(coords, vectors, bases, transfer, coupling, top_transfer, top_coupling):
    vectors = vectors.T
    device = lax.axis_index(AXES).astype(jnp.int32).reshape(1)
    climbing, table0, table1, table2, levels, pairs, quads = upward(
        device,
        bases.transpose(1, 2, 0),
        vectors,
        transfer[0].transpose(1, 2, 0),
        top_transfer.transpose(1, 2, 0),
        top_coupling.transpose(1, 2, 0),
    )
    coupling = coupling[0]
    partners, nears, lows = [], [None] * 4, []
    for height, mask in enumerate(MASKS):
        partner = exchanged(climbing, mask)
        if height == 0:
            own0, sib0 = first_pick(climbing, device, table0)
            own, sib = [own0], [sib0]
        elif height == 1:
            owns, sibs = second_pick(climbing, device, table1)
            own += [owns[n] for n in range(6)]
            sib += [sibs[n] for n in range(6)]
        elif height == 3:
            lift = lifts(climbing, device, own0, owns, table2)
        elif height == 4:
            state = upper(climbing, coupling, levels, quads)
        for piece in NEAR_BESIDE.get(height, ()):
            nears[piece] = near(piece, climbing, coords, vectors)
        for piece in BESIDE.get(height, ()):
            lows.append(
                lower_piece(piece, climbing, state, nears[piece], coupling, levels, quads, pairs)
            )
        if height == 7:
            partial = partial_field(climbing, lift, partners)
        partners.append(partner)
        if height < 7:
            climbing = dot(climbing, own[height]) + dot(partner, sib[height])
    result = final(lift, partial, partner, [low[0] for low in lows], [low[1] for low in lows])
    return result.T


def solution(mesh):
    both = ("leaf", "sub")
    return jax.shard_map(
        on_device,
        mesh=mesh,
        in_specs=(
            P(None, both),
            P(both, None),
            P(both, None, None),
            P(both, None, None, None),
            P(both, None, None, None),
            P(),
            P(),
        ),
        out_specs=P(both, None),
        check_vma=False,
    )
```

```python
import functools

import jax
import jax.numpy as jnp
from jax import lax
from jax.experimental import pallas as pl
from jax.experimental.pallas import tpu as pltpu
from jax.sharding import PartitionSpec as P

F32 = jnp.float32
BF16 = jnp.bfloat16
VMEM = pltpu.VMEM
AXES = ("leaf", "sub")
HIGH = lax.Precision.HIGHEST

STEP = 136
NN = (((1,), (0,)), ((), ()))
NT = (((1,), (1,)), ((), ()))
LEVEL_AT = (None, 0, 4096, 6144, 7168, 7680, 7936)
NODE_AT = (0, 128, 192, 224, 240, 248, 252)
NUGGET_DIAG = 1.5
CHORD = 2.0 * 1.4426950408889634


def mxu(a, b, dims):
    return lax.dot_general(a, b, dims, preferred_element_type=F32)


def split(c):
    hi = c.astype(BF16)
    lo = (c - hi.astype(F32)).astype(BF16)
    return jnp.concatenate([hi, lo], 0)


def fold(t):
    half = t.shape[0] // 2
    return t[:half] + t[half:]


def half_mask():
    return lax.broadcasted_iota(jnp.int32, (32, 128), 1) < 64


def spread(src, width, lane0, slab, rows):
    for i in rows:
        w = jnp.concatenate([src[i, :, lane0 : lane0 + width], src[i + 32, :, lane0 : lane0 + width]], 0)
        if width < 128:
            w = jnp.concatenate([w, jnp.zeros((128, 128 - width), BF16)], 1)
        slab[pl.ds(i * STEP, 128), :] = w.T.astype(F32)


def box_matrix(slab, box, right, low):
    x = slab[pl.ds(box, 32, stride=STEP), :]
    y = pltpu.roll(x, 64, 1)
    if right:
        return jnp.concatenate([jnp.where(low, 0.0, y), jnp.where(low, 0.0, x)], 0)
    return jnp.concatenate([jnp.where(low, x, 0.0), jnp.where(low, y, 0.0)], 0)


def up_kernel(
    device, bases_h, vectors_h, transfer_h, top_transfer_h,
    own_out, table0, table1, levels_h, pairs_h, quads_h,
    bases, vectors, transfer, slab0, slab1, slab2, leaf_coef, levels, pairs, quads, sems, out_sems,
):
    loads = []
    for k in range(4):
        part = pl.ds(16 * (k // 2) + 32 * (k % 2), 16)
        loads.append(pltpu.make_async_copy(bases_h.at[part], bases.at[part], sems.at[k]))
    loads.append(pltpu.make_async_copy(vectors_h, vectors, sems.at[4]))
    loads.append(pltpu.make_async_copy(transfer_h, transfer, sems.at[5]))
    lane0 = pl.multiple_of(128 * (device[0] >> 7), 128)
    tables = [
        (top_transfer_h.at[:, :, pl.ds(lane0, 128)], table0),
        (top_transfer_h.at[:, :, pl.ds(256, 252)], table1),
    ]
    loads += [
        pltpu.make_async_copy(src, dst, sems.at[6 + n]) for n, (src, dst) in enumerate(tables)
    ]
    for copy in loads:
        copy.start()
    stores = []

    def store(src, dst):
        copy = pltpu.make_async_copy(src, dst, out_sems.at[len(stores)])
        copy.start()
        stores.append(copy)

    low = half_mask()
    for k in range(2):
        loads[2 * k].wait()
        loads[2 * k + 1].wait()
        spread(bases, 128, 0, slab0, range(16 * k, 16 * k + 16))
    loads[4].wait()
    held = []
    for j in range(64 + DEPTH):
        if j == 16:
            loads[5].wait()
        if j < 64:
            pair = jnp.concatenate(
                [box_matrix(slab0, 2 * j, False, low), box_matrix(slab0, 2 * j + 1, True, low)], 0
            ).astype(BF16)
            pairs[j] = pair
            held.append(pair)
        if 16 <= j < 48:
            spread(transfer, 128, 0, slab1, [j - 16])
        if j >= DEPTH:
            at = 128 * (j - DEPTH)
            leaf_coef[:, at : at + 128] = mxu(vectors[:, at : at + 128], held[j - DEPTH], NN)
    store(pairs, pairs_h)
    steps = [(level, q) for level in range(6) for q in range((128 >> level) // 4)]
    held = []
    for k in range(len(steps) + UP_DEPTH):
        if k < 16:
            spread(transfer, 126, 128, slab2, [2 * k, 2 * k + 1])
        if k < len(steps):
            level, q = steps[k]
            first = NODE_AT[level] + 4 * q
            slab = slab1 if first < 128 else slab2
            quad = jnp.concatenate(
                [box_matrix(slab, (first + u) % 128, u >= 2, low) for u in range(4)], 0
            ).astype(BF16)
            quads[first // 4] = quad
            held.append(quad)
        if k >= UP_DEPTH:
            level, q = steps[k - UP_DEPTH]
            count = 128 >> level
            if level == 0:
                coef = leaf_coef[:, 256 * q : 256 * q + 256]
            else:
                at = LEVEL_AT[level] + 256 * q
                coef = levels[:, at : at + 256]
            at = LEVEL_AT[level + 1] + 128 * q
            levels[:, at : at + 128] = fold(mxu(split(coef), held[k - UP_DEPTH], NN))
            if level < 2 and q == count // 4 - 1:
                part = pl.ds(NODE_AT[level] // 4, count // 4)
                store(quads.at[part], quads_h.at[part])
                if level == 1:
                    part = pl.ds(LEVEL_AT[2], 2048)
                    store(levels.at[:, part], levels_h.at[:, pl.ds(0, 2048)])
    last = jnp.concatenate(
        [box_matrix(slab2, 124, False, low), box_matrix(slab2, 125, False, low)], 0
    ).astype(BF16)
    quads[63, :128, :] = last
    quads[63, 128:, :] = jnp.zeros((128, 128), BF16)
    part = pl.ds(48, 16)
    store(quads.at[part], quads_h.at[part])
    part = pl.ds(LEVEL_AT[3], 1920)
    store(levels.at[:, part], levels_h.at[:, pl.ds(2048, 1920)])
    at = LEVEL_AT[6]
    own_out[...] = fold(mxu(split(levels[:, at : at + 128]), last, NN))[:, :64]
    for copy in loads[6:] + stores:
        copy.wait()


def params(mib):
    return pltpu.CompilerParams(vmem_limit_bytes=mib * 2**20)


def cost(us):
    return pl.CostEstimate(flops=int(us * 10**9), bytes_accessed=2**16, transcendentals=0)


UP_MIB = 52
WINDOW_MIB = 12
UP_DEPTH = 4
DEPTH = 2
IN_VMEM = pl.BlockSpec(memory_space=VMEM)
IN_HBM = pl.BlockSpec(memory_space=pl.ANY)
IN_SMEM = pl.BlockSpec(memory_space=pltpu.SMEM)


def upward(device, bases, vectors, transfer, top_transfer):
    return pl.pallas_call(
        up_kernel,
        out_shape=[
            jax.ShapeDtypeStruct((64, 64), F32),
            jax.ShapeDtypeStruct((64, 64, 128), BF16),
            jax.ShapeDtypeStruct((64, 64, 252), BF16),
            jax.ShapeDtypeStruct((64, 3968), F32),
            jax.ShapeDtypeStruct((64, 128, 128), BF16),
            jax.ShapeDtypeStruct((64, 256, 128), BF16),
        ],
        in_specs=[IN_SMEM] + [IN_HBM] * 4,
        out_specs=[IN_VMEM] * 3 + [IN_HBM] * 3,
        scratch_shapes=[
            VMEM((64, 64, 128), BF16),
            VMEM((64, 8192), BF16),
            VMEM((64, 64, 254), BF16),
            VMEM((32 * STEP, 128), F32),
            VMEM((32 * STEP, 128), F32),
            VMEM((32 * STEP, 128), F32),
            VMEM((64, 8192), F32),
            VMEM((64, 8064), F32),
            VMEM((64, 128, 128), BF16),
            VMEM((64, 256, 128), BF16),
            pltpu.SemaphoreType.DMA((8,)),
            pltpu.SemaphoreType.DMA((7,)),
        ],
        compiler_params=params(UP_MIB),
        cost_estimate=cost(8),
        name="upward",
    )(device, bases, vectors, transfer, top_transfer)


def pick_rows(table, pick, slab):
    for i in range(16):
        rows = jnp.concatenate(
            [table[2 * i], table[2 * i + 32], table[2 * i + 1], table[2 * i + 33]], 0
        )
        out = mxu(pick, rows, NT)
        slab[pl.ds(48 * i, 16), :] = out[:, :128]
        slab[pl.ds(48 * i + 24, 16), :] = out[:, 128:]


def picked(slab, row):
    x = slab[pl.ds(row, 32, stride=24), :]
    return jnp.concatenate([x, pltpu.roll(x, 64, 1)], 0)[:, :64]


def transfer_pick(dev, heights, lane0, width):
    row = lax.broadcasted_iota(jnp.int32, (16, width), 0)
    col = lax.broadcasted_iota(jnp.int32, (16, width), 1)
    hit = jnp.zeros((16, width), jnp.bool_)
    for n, height in enumerate(heights):
        box = 512 - (512 >> height) + (dev >> height) - lane0
        hit = hit | ((row == n) & (col == box))
        hit = hit | ((row == n + 8) & (col == (box ^ 1)))
        if height in (1, 6):
            extra = 6 if height == 1 else 14
            hit = hit | ((row == extra) & (col == (box ^ 2)))
            hit = hit | ((row == extra + 1) & (col == (box ^ 3)))
    return jnp.where(hit, 1.0, 0.0).astype(BF16)


def thirds(x):
    a = x.astype(BF16).astype(F32)
    b = (x - a).astype(BF16).astype(F32)
    return a, b, x - a - b


def near_field(piece, coords, vectors, out, square_x, left_t, right):
    square_x[0:3, :] = coords[:, 2048 * piece : 2048 * piece + 2048] * CHORD
    square_x[3:8, :] = jnp.zeros((5, 2048), F32)
    x = square_x[...]
    one8 = jnp.where(lax.broadcasted_iota(jnp.int32, (8, 2048), 0) == 0, 1.0, 0.0)
    x1, x2, x3 = thirds(x)
    n1, n2, n3 = thirds(jnp.sum(x * x, axis=0, keepdims=True) * one8)
    left = jnp.concatenate([x1, x1, x2, x2, x1, x3, n1, n2, n3, one8, one8, one8], 0)
    left_t[...] = left.astype(BF16).T
    y1, y2, y3 = -2 * x1, -2 * x2, -2 * x3
    right[...] = jnp.concatenate(
        [y1, y2, y1, y2, y3, y1, one8, one8, one8, n1, n2, n3], 0
    ).astype(BF16)
    eye = (
        lax.broadcasted_iota(jnp.int32, (128, 128), 0)
        == lax.broadcasted_iota(jnp.int32, (128, 128), 1)
    )
    held = []

    def apply(at, side, first, second):
        here = 2048 * piece + at
        v0 = vectors[:, here : here + 128]
        v1 = vectors[:, here + 128 : here + 256]
        out[:, at : at + 128] = mxu(v0, first, NN) + mxu(v1, side, NT)
        out[:, at + 128 : at + 256] = mxu(v0, side, NN) + mxu(v1, second, NN)

    for g in range(8 + DEPTH):
        if g < 8:
            at = 256 * g

            def block(a, b):
                square = mxu(left_t[at + a : at + a + 128, :], right[:, at + b : at + b + 128], NN)
                square = jnp.maximum(square, 1e-30)
                value = jnp.exp2(-(square * lax.rsqrt(square)))
                if a == b:
                    value = jnp.where(eye, NUGGET_DIAG, value)
                return value.astype(BF16)

            held.append((at, block(0, 128), block(0, 0), block(128, 128)))
        if g >= DEPTH:
            apply(*held[g - DEPTH])


NEAR_SCRATCH = [
    VMEM((8, 2048), F32),
    VMEM((2048, 96), BF16),
    VMEM((96, 2048), BF16),
]


def first_kernel(after, device, transfer, own_out, sib_out, slab):
    dev = device[0]
    lane0 = pl.multiple_of(128 * (dev >> 7), 128)
    pick_rows(transfer, transfer_pick(dev, [0], lane0, 128), slab)
    own_out[...] = picked(slab, 0)
    sib_out[...] = picked(slab, 8)


def first_pick(after, device, transfer):
    return pl.pallas_call(
        first_kernel,
        out_shape=[jax.ShapeDtypeStruct((64, 64), F32)] * 2,
        in_specs=[IN_VMEM, IN_SMEM, IN_VMEM],
        out_specs=[IN_VMEM] * 2,
        scratch_shapes=[VMEM((32 * 24, 128), F32)],
        compiler_params=params(WINDOW_MIB),
        cost_estimate=cost(1),
        name="first_pick",
    )(after, device, transfer)


def second_kernel(after, device, transfer, own_out, sib_out, quad_out, slab):
    dev = device[0]
    pick_rows(transfer, transfer_pick(dev, range(1, 7), 256, 252), slab)
    rows = [picked(slab, n) for n in range(16)]
    for n in range(6):
        own_out[n] = rows[n]
        sib_out[n] = rows[8 + n]
    own_out[6] = rows[14]
    own_out[7] = rows[15]
    up = [rows[1].astype(BF16), rows[9].astype(BF16)]
    for n, (row, side) in enumerate([(0, 0), (8, 0), (6, 1), (7, 1)]):
        quad_out[n] = mxu(rows[row].astype(BF16), up[side], NN)
    quad_out[4] = rows[6]
    quad_out[5] = rows[7]


def second_pick(after, device, transfer):
    return pl.pallas_call(
        second_kernel,
        out_shape=[
            jax.ShapeDtypeStruct((8, 64, 64), F32),
            jax.ShapeDtypeStruct((6, 64, 64), F32),
            jax.ShapeDtypeStruct((6, 64, 64), F32),
        ],
        in_specs=[IN_VMEM, IN_SMEM, IN_VMEM],
        out_specs=[IN_VMEM] * 3,
        scratch_shapes=[VMEM((32 * 24, 128), F32)],
        compiler_params=params(WINDOW_MIB),
        cost_estimate=cost(1),
        name="second_pick",
    )(after, device, transfer)


def combine_kernel(quad, own, a, b, c, up_out, sib_out):
    blocks = [own[...], a[...], b[...], c[...]]
    terms = [field_term(x, quad[n]) for n, x in enumerate(blocks)]
    up_out[...] = (terms[0] + terms[1]) + (terms[2] + terms[3])
    sib_out[...] = field_term(b[...], quad[4]) + field_term(c[...], quad[5])


def combine(quad, own, a, b, c):
    return pl.pallas_call(
        combine_kernel,
        out_shape=[jax.ShapeDtypeStruct((64, 64), F32)] * 2,
        in_specs=[IN_VMEM] * 5,
        out_specs=[IN_VMEM] * 2,
        compiler_params=params(WINDOW_MIB),
        cost_estimate=cost(0.3),
        name="combine",
    )(quad, own, a, b, c)


def lift_kernel(after, device, own0, own, table, lift_out, slab):
    dev = device[0]
    row = lax.broadcasted_iota(jnp.int32, (16, 255), 0)
    col = lax.broadcasted_iota(jnp.int32, (16, 255), 1)
    want = 256 - (256 >> row) + (jnp.full_like(row, dev) >> (row + 1))
    pick_rows(table, jnp.where((col == want) & (row < 8), 1.0, 0.0).astype(BF16), slab)
    turned = []
    for level in range(8):
        pair = picked(slab, level)
        odd = (dev >> level) & 1
        turned.append(jnp.where(odd == 1, pair, pair.T).astype(BF16))
    steps = [own0[...].T] + [own[n].T.astype(BF16) for n in range(6)]
    lift_out[0] = turned[0].astype(F32)
    chain = steps[0]
    for level in range(1, 8):
        hi = chain.astype(BF16)
        lo = (chain - hi.astype(F32)).astype(BF16)
        if level < 7:
            chain = mxu(steps[level], hi, NN) + mxu(steps[level], lo, NN)
        last = mxu(turned[level], hi, NN) + mxu(turned[level], lo, NN)
        if level < 7:
            lift_out[level] = last
    hi = last.astype(BF16)
    lo = (last - hi.astype(F32)).astype(BF16)
    for n in range(2):
        e = own[6 + n].astype(BF16)
        lift_out[7 + n] = mxu(e, hi, NN) + mxu(e, lo, NN)


def lifts(after, device, own0, own, coupling):
    return pl.pallas_call(
        lift_kernel,
        out_shape=jax.ShapeDtypeStruct((9, 64, 64), F32),
        in_specs=[IN_VMEM, IN_SMEM, IN_VMEM, IN_VMEM, IN_VMEM],
        out_specs=IN_VMEM,
        scratch_shapes=[VMEM((32 * 24, 128), F32)],
        compiler_params=params(WINDOW_MIB),
        cost_estimate=cost(2),
        name="lifts",
    )(after, device, own0, own, coupling)


def near_kernel(piece, after, coords, vectors, near_out, square_x, left_t, right):
    near_field(piece, coords, vectors, near_out, square_x, left_t, right)


def near(piece, after, coords, vectors):
    return pl.pallas_call(
        functools.partial(near_kernel, piece),
        out_shape=jax.ShapeDtypeStruct((64, 2048), F32),
        in_specs=[IN_VMEM] * 3,
        out_specs=IN_VMEM,
        scratch_shapes=NEAR_SCRATCH,
        compiler_params=params(WINDOW_MIB),
        cost_estimate=cost(1.5),
        name="near",
    )(after, coords, vectors)


def shift_right():
    row = lax.broadcasted_iota(jnp.int32, (64, 128), 0)
    col = lax.broadcasted_iota(jnp.int32, (64, 128), 1)
    return jnp.where(col == row + 64, 1.0, 0.0).astype(BF16)


def pair_fields(coefs, couplings, shift):
    blank = jnp.zeros((64, 128), BF16)
    sides = [jnp.concatenate([mxu(c[...], shift, NN).astype(BF16), blank], 0) for c in couplings]
    parts = [split(c[...]) for c in coefs]
    terms = [(mxu(s, z, NN), mxu(s, z, NT)) for s, z in zip(parts, sides)]
    return [fold(a + b) for a, b in terms]


def with_fields(state, fields):
    return jnp.concatenate([state[:64] + jnp.concatenate(fields, 1), state[64:]], 0)


def descend(state, quad):
    return fold(mxu(split(state), quad, NT))


def upper_kernel(after, coupling, levels, quads, state_out):
    shift = shift_right()

    where = [(level, pair) for level in range(6, 2, -1) for pair in range((64 >> level))]
    found = pair_fields(
        [levels.at[:, pl.ds(LEVEL_AT[level] - 4096 + 128 * pair, 128)] for level, pair in where],
        [coupling.at[32 - (32 >> (level - 2)) + pair] for level, pair in where],
        shift,
    )
    found = dict(zip(where, found))

    def field(level, pair):
        return found[level, pair]

    unit = jnp.where(
        lax.broadcasted_iota(jnp.int32, (64, 64), 0)
        == lax.broadcasted_iota(jnp.int32, (64, 64), 1),
        1.0,
        0.0,
    ).astype(BF16)
    state = jnp.concatenate([field(6, 0), mxu(unit, quads[63, :128, :64], NT)], 0)
    for level in range(5, 2, -1):
        below = []
        for q in range((128 >> level) // 4):
            s = descend(state[:, 128 * q : 128 * q + 128], quads[NODE_AT[level] // 4 + q])
            below.append(with_fields(s, [field(level, 2 * q), field(level, 2 * q + 1)]))
        state = jnp.concatenate(below, 1)
    state_out[...] = state


def upper(after, coupling, levels, quads):
    return pl.pallas_call(
        upper_kernel,
        out_shape=jax.ShapeDtypeStruct((128, 1024), F32),
        in_specs=[IN_VMEM] * 4,
        out_specs=IN_VMEM,
        compiler_params=params(WINDOW_MIB),
        cost_estimate=cost(1.5),
        name="upper",
    )(after, coupling, levels, quads)


def lower_kernel(piece, after, state3, near_in, coupling, levels, quads, pairs, base_out, top_out):
    shift = shift_right()
    mine = range(4 * piece, 4 * piece + 4)
    fields = pair_fields(
        [levels.at[:, pl.ds(128 * p, 128)] for p in mine],
        [coupling.at[p] for p in mine],
        shift,
    )
    state = state3[:, 256 * piece : 256 * piece + 256]
    state = jnp.concatenate(
        [
            with_fields(
                descend(state[:, 128 * q : 128 * q + 128], quads[48 + 2 * piece + q]),
                fields[2 * q : 2 * q + 2],
            )
            for q in range(2)
        ],
        1,
    )
    state = jnp.concatenate(
        [descend(state[:, 128 * q : 128 * q + 128], quads[32 + 4 * piece + q]) for q in range(4)], 1
    )
    leaves = []
    for q in range(8 + DEPTH):
        if q < 8:
            leaves.append(descend(state[:, 128 * q : 128 * q + 128], quads[8 * piece + q]))
        if q >= DEPTH:
            for u in range(2):
                pair = 2 * (q - DEPTH) + u
                at = 128 * pair
                t = descend(
                    leaves[q - DEPTH][:, 128 * u : 128 * u + 128], pairs[16 * piece + pair]
                )
                base_out[:, at : at + 128] = t[:64] + near_in[:, at : at + 128]
                top_out[:, at : at + 128] = split(t[64:])


def lower_piece(piece, after, state3, near_in, coupling, levels, quads, pairs):
    return pl.pallas_call(
        functools.partial(lower_kernel, piece),
        out_shape=[
            jax.ShapeDtypeStruct((64, 2048), F32),
            jax.ShapeDtypeStruct((128, 2048), BF16),
        ],
        in_specs=[IN_VMEM] * 7,
        out_specs=[IN_VMEM] * 2,
        compiler_params=params(WINDOW_MIB),
        cost_estimate=cost(1.5),
        name="lower",
    )(after, state3, near_in, coupling, levels, quads, pairs)


def field_term(partner, lift):
    hi = lift.astype(BF16)
    lo = (lift - hi.astype(F32)).astype(BF16)
    p = split(partner)
    return fold(mxu(p, hi, NN)) + mxu(p[:64], lo, NN)


def partial_kernel(after, lift, *refs):
    terms = [field_term(refs[height][...], lift[height]) for height in range(6)]
    refs[6][...] = sum(terms[1:], terms[0])


def partial_field(after, lift, partners):
    return pl.pallas_call(
        partial_kernel,
        out_shape=jax.ShapeDtypeStruct((64, 64), F32),
        in_specs=[IN_VMEM] * 8,
        out_specs=IN_VMEM,
        compiler_params=params(WINDOW_MIB),
        cost_estimate=cost(0.5),
        name="partial_field",
    )(after, lift, *partners)


def final_kernel(lift, partial, *refs):
    bases = refs[3:7]
    tops = refs[7:11]
    out_h, out, sems = refs[11:]
    terms = [field_term(refs[n][...], lift[6 + n]) for n in range(3)]
    g = (partial[...] + terms[0]) + (terms[1] + terms[2])
    hi = g.astype(BF16)
    lo = (g - hi.astype(F32)).astype(BF16)
    g = jnp.concatenate(
        [jnp.concatenate([hi, hi], 1), jnp.concatenate([lo, jnp.zeros_like(lo)], 1)], 0
    )
    copies = []
    for piece in range(4):
        for q in range(8):
            at = 256 * q
            out[:, 2048 * piece + at : 2048 * piece + at + 256] = (
                fold(mxu(g, tops[piece][:, at : at + 256], NN)) + bases[piece][:, at : at + 256]
            )
        part = pl.ds(2048 * piece, 2048)
        copies.append(pltpu.make_async_copy(out.at[:, part], out_h.at[:, part], sems.at[piece]))
        copies[-1].start()
    for copy in copies:
        copy.wait()


def final(lift, partial, partners, bases, tops):
    return pl.pallas_call(
        final_kernel,
        out_shape=jax.ShapeDtypeStruct((64, 8192), F32),
        in_specs=[IN_VMEM] * 13,
        out_specs=IN_HBM,
        scratch_shapes=[VMEM((64, 8192), F32), pltpu.SemaphoreType.DMA((4,))],
        compiler_params=params(16),
        cost_estimate=cost(2),
        name="final",
    )(lift, partial, *partners, *bases, *tops)


def exchanged(value, mask):
    devices = lax.axis_size(AXES)
    return lax.ppermute(value, AXES, [(s, s ^ mask) for s in range(devices)])


def dot(a, b):
    return jnp.dot(a, b, precision=HIGH)


def on_device(coords, vectors, bases, transfer, coupling, top_transfer, top_coupling):
    vectors = vectors.T
    device = lax.axis_index(AXES).astype(jnp.int32).reshape(1)
    climbing, table0, table1, levels, pairs, quads = upward(
        device,
        bases.transpose(1, 2, 0),
        vectors,
        transfer[0].transpose(1, 2, 0),
        top_transfer.transpose(1, 2, 0),
    )
    table2 = top_coupling.transpose(1, 2, 0)
    coupling = coupling[0]
    lows = []

    def lower_with(after, piece, near_in):
        lows.append(lower_piece(piece, after, state, near_in, coupling, levels, quads, pairs))

    fields = [exchanged(climbing, 1)]
    own0, sib0 = first_pick(climbing, device, table0)
    climbing = dot(climbing, own0) + dot(fields[0], sib0)
    start = climbing
    owns, sibs, quad = second_pick(start, device, table1)
    ring = [exchanged(start, mask) for mask in (2, 4, 6)]
    near0 = near(0, start, coords, vectors)
    near1 = near(1, start, coords, vectors)
    climbing, sibling = combine(quad, start, *ring)
    fields += [ring[0], sibling]
    for height, mask in ((3, 8), (4, 16), (5, 48)):
        start = climbing
        fields.append(exchanged(start, mask))
        if height == 3:
            lift = lifts(start, device, own0, owns, table2)
            near2 = near(2, start, coords, vectors)
        elif height == 4:
            state = upper(start, coupling, levels, quads)
            lower_with(start, 0, near0)
        else:
            near3 = near(3, start, coords, vectors)
            lower_with(start, 1, near1)
        climbing = dot(start, owns[height - 1]) + dot(fields[-1], sibs[height - 1])
    ring = [exchanged(climbing, mask) for mask in (64, 128, 192)]
    lower_with(climbing, 2, near2)
    lower_with(climbing, 3, near3)
    partial = partial_field(climbing, lift, fields)
    result = final(lift, partial, ring, [low[0] for low in lows], [low[1] for low in lows])
    return result.T


def solution(mesh):
    both = ("leaf", "sub")
    return jax.shard_map(
        on_device,
        mesh=mesh,
        in_specs=(
            P(None, both),
            P(both, None),
            P(both, None, None),
            P(both, None, None, None),
            P(both, None, None, None),
            P(),
            P(),
        ),
        out_specs=P(both, None),
        check_vma=False,
    )
```

```python
import functools

import jax
import jax.numpy as jnp
from jax import lax
from jax.experimental import pallas as pl
from jax.experimental.pallas import tpu as pltpu
from jax.sharding import PartitionSpec as P

F32 = jnp.float32
BF16 = jnp.bfloat16
VMEM = pltpu.VMEM
AXES = ("leaf", "sub")

STEP = 136
NN = (((1,), (0,)), ((), ()))
NT = (((1,), (1,)), ((), ()))
LEVEL_AT = (None, 0, 4096, 6144, 7168, 7680, 7936)
NODE_AT = (0, 128, 192, 224, 240, 248, 252)
NUGGET_DIAG = 1.5
CHORD = 2.0 * 1.4426950408889634


def mxu(a, b, dims):
    return lax.dot_general(a, b, dims, preferred_element_type=F32)


def split(c):
    hi = c.astype(BF16)
    lo = (c - hi.astype(F32)).astype(BF16)
    return jnp.concatenate([hi, lo], 0)


def fold(t):
    half = t.shape[0] // 2
    return t[:half] + t[half:]


def half_mask():
    return lax.broadcasted_iota(jnp.int32, (32, 128), 1) < 64


def spread(src, width, lane0, slab, rows):
    for i in rows:
        w = jnp.concatenate([src[i, :, lane0 : lane0 + width], src[i + 32, :, lane0 : lane0 + width]], 0)
        if width < 128:
            w = jnp.concatenate([w, jnp.zeros((128, 128 - width), BF16)], 1)
        slab[pl.ds(i * STEP, 128), :] = w.T.astype(F32)


def box_matrix(slab, box, right, low):
    x = slab[pl.ds(box, 32, stride=STEP), :]
    y = pltpu.roll(x, 64, 1)
    if right:
        return jnp.concatenate([jnp.where(low, 0.0, y), jnp.where(low, 0.0, x)], 0)
    return jnp.concatenate([jnp.where(low, x, 0.0), jnp.where(low, y, 0.0)], 0)


def up_kernel(
    device, bases_h, vectors_h, transfer_h, top_transfer_h,
    own_out, own0_out, sib0_out, levels, quads_top, pairs_h, quads_h,
    bases, vectors, transfer, slab0, slab1, slab2, leaf_coef, level1, pairs, quads, table0, picks, sems, out_sems,
):
    loads = []
    for k in range(4):
        part = pl.ds(16 * (k // 2) + 32 * (k % 2), 16)
        loads.append(pltpu.make_async_copy(bases_h.at[part], bases.at[part], sems.at[k]))
    loads.append(pltpu.make_async_copy(vectors_h, vectors, sems.at[4]))
    loads.append(pltpu.make_async_copy(transfer_h, transfer, sems.at[5]))
    lane0 = pl.multiple_of(128 * (device[0] >> 7), 128)
    loads.append(
        pltpu.make_async_copy(top_transfer_h.at[:, :, pl.ds(lane0, 128)], table0, sems.at[6])
    )
    for copy in loads:
        copy.start()
    stores = []

    def store(src, dst):
        copy = pltpu.make_async_copy(src, dst, out_sems.at[len(stores)])
        copy.start()
        stores.append(copy)

    low = half_mask()
    for k in range(2):
        loads[2 * k].wait()
        loads[2 * k + 1].wait()
        spread(bases, 128, 0, slab0, range(16 * k, 16 * k + 16))
    loads[4].wait()
    held = []
    for j in range(64 + DEPTH):
        if j == 16:
            loads[5].wait()
        if j < 64:
            pair = jnp.concatenate(
                [box_matrix(slab0, 2 * j, False, low), box_matrix(slab0, 2 * j + 1, True, low)], 0
            ).astype(BF16)
            pairs[j] = pair
            held.append(pair)
        if 16 <= j < 48:
            spread(transfer, 128, 0, slab1, [j - 16])
        if j >= DEPTH:
            at = 128 * (j - DEPTH)
            leaf_coef[:, at : at + 128] = mxu(vectors[:, at : at + 128], held[j - DEPTH], NN)
    store(pairs, pairs_h)
    steps = [(level, q) for level in range(6) for q in range((128 >> level) // 4)]
    held = []
    for k in range(len(steps) + UP_DEPTH):
        if k < 16:
            spread(transfer, 126, 128, slab2, [2 * k, 2 * k + 1])
        if k == 47:
            loads[6].wait()
            first_pick = transfer_pick(device[0], [0], lane0, 128)
        if 47 <= k < 63:
            pick_row(table0, first_pick, picks, k - 47)
        if k < len(steps):
            level, q = steps[k]
            first = NODE_AT[level] + 4 * q
            slab = slab1 if first < 128 else slab2
            quad = jnp.concatenate(
                [box_matrix(slab, (first + u) % 128, u >= 2, low) for u in range(4)], 0
            ).astype(BF16)
            if level < 3:
                quads[first // 4] = quad
                if q == (32 >> level) - 1:
                    part = pl.ds(NODE_AT[level] // 4, 32 >> level)
                    store(quads.at[part], quads_h.at[part])
            else:
                quads_top[first // 4 - 56] = quad
            held.append(quad)
        if k >= UP_DEPTH:
            level, q = steps[k - UP_DEPTH]
            if level == 0:
                coef = leaf_coef[:, 256 * q : 256 * q + 256]
            elif level == 1:
                coef = level1[:, 256 * q : 256 * q + 256]
            else:
                at = LEVEL_AT[level] - 4096 + 256 * q
                coef = levels[:, at : at + 256]
            coef = fold(mxu(split(coef), held[k - UP_DEPTH], NN))
            if level == 0:
                level1[:, 128 * q : 128 * q + 128] = coef
            else:
                at = LEVEL_AT[level + 1] - 4096 + 128 * q
                levels[:, at : at + 128] = coef
    last = jnp.concatenate(
        [box_matrix(slab2, 124, False, low), box_matrix(slab2, 125, False, low)], 0
    ).astype(BF16)
    quads_top[7, :128, :] = last
    quads_top[7, 128:, :] = jnp.zeros((128, 128), BF16)
    at = LEVEL_AT[6] - 4096
    own_out[...] = fold(mxu(split(levels[:, at : at + 128]), last, NN))[:, :64]
    own0_out[...] = picked(picks, 0)
    sib0_out[...] = picked(picks, 8)
    for copy in stores:
        copy.wait()


def params(mib):
    return pltpu.CompilerParams(vmem_limit_bytes=mib * 2**20)


def cost(us):
    return pl.CostEstimate(flops=int(us * 10**9), bytes_accessed=2**16, transcendentals=0)


UP_MIB = 52
WINDOW_MIB = 12
UP_DEPTH = 4
DEPTH = 2
IN_VMEM = pl.BlockSpec(memory_space=VMEM)
IN_HBM = pl.BlockSpec(memory_space=pl.ANY)
IN_SMEM = pl.BlockSpec(memory_space=pltpu.SMEM)


def upward(device, bases, vectors, transfer, top_transfer):
    return pl.pallas_call(
        up_kernel,
        out_shape=[
            jax.ShapeDtypeStruct((64, 64), F32),
            jax.ShapeDtypeStruct((64, 64), F32),
            jax.ShapeDtypeStruct((64, 64), F32),
            jax.ShapeDtypeStruct((64, 3968), F32),
            jax.ShapeDtypeStruct((8, 256, 128), BF16),
            jax.ShapeDtypeStruct((64, 128, 128), BF16),
            jax.ShapeDtypeStruct((56, 256, 128), BF16),
        ],
        in_specs=[IN_SMEM] + [IN_HBM] * 4,
        out_specs=[IN_VMEM] * 5 + [IN_HBM] * 2,
        scratch_shapes=[
            VMEM((64, 64, 128), BF16),
            VMEM((64, 8192), BF16),
            VMEM((64, 64, 254), BF16),
            VMEM((32 * STEP, 128), F32),
            VMEM((32 * STEP, 128), F32),
            VMEM((32 * STEP, 128), F32),
            VMEM((64, 8192), F32),
            VMEM((64, 4096), F32),
            VMEM((64, 128, 128), BF16),
            VMEM((56, 256, 128), BF16),
            VMEM((64, 64, 128), BF16),
            VMEM((32 * 24, 128), F32),
            pltpu.SemaphoreType.DMA((7,)),
            pltpu.SemaphoreType.DMA((4,)),
        ],
        compiler_params=params(UP_MIB),
        cost_estimate=cost(8),
        name="upward",
    )(device, bases, vectors, transfer, top_transfer)


def pick_row(table, pick, slab, i):
    rows = jnp.concatenate(
        [table[2 * i], table[2 * i + 32], table[2 * i + 1], table[2 * i + 33]], 0
    )
    out = mxu(pick, rows, NT)
    slab[pl.ds(48 * i, 16), :] = out[:, :128]
    slab[pl.ds(48 * i + 24, 16), :] = out[:, 128:]


def pick_rows(table, pick, slab):
    for i in range(16):
        pick_row(table, pick, slab, i)


def picked(slab, row):
    x = slab[pl.ds(row, 32, stride=24), :]
    return jnp.concatenate([x, pltpu.roll(x, 64, 1)], 0)[:, :64]


def transfer_pick(dev, heights, lane0, width):
    row = lax.broadcasted_iota(jnp.int32, (16, width), 0)
    col = lax.broadcasted_iota(jnp.int32, (16, width), 1)
    hit = jnp.zeros((16, width), jnp.bool_)
    for n, height in enumerate(heights):
        box = 512 - (512 >> height) + (dev >> height) - lane0
        hit = hit | ((row == n) & (col == box))
        hit = hit | ((row == n + 8) & (col == (box ^ 1)))
        if height in (1, 6):
            extra = 6 if height == 1 else 14
            hit = hit | ((row == extra) & (col == (box ^ 2)))
            hit = hit | ((row == extra + 1) & (col == (box ^ 3)))
    return jnp.where(hit, 1.0, 0.0).astype(BF16)


def thirds(x):
    a = x.astype(BF16).astype(F32)
    b = (x - a).astype(BF16).astype(F32)
    return a, b, x - a - b


def near_field(piece, coords, vectors, out, square_x, left_t, right):
    square_x[0:3, :] = coords[:, 2048 * piece : 2048 * piece + 2048] * CHORD
    square_x[3:8, :] = jnp.zeros((5, 2048), F32)
    x = square_x[...]
    one8 = jnp.where(lax.broadcasted_iota(jnp.int32, (8, 2048), 0) == 0, 1.0, 0.0)
    x1, x2, x3 = thirds(x)
    n1, n2, n3 = thirds(jnp.sum(x * x, axis=0, keepdims=True) * one8)
    left = jnp.concatenate([x1, x1, x2, x2, x1, x3, n1, n2, n3, one8, one8, one8], 0)
    left_t[...] = left.astype(BF16).T
    y1, y2, y3 = -2 * x1, -2 * x2, -2 * x3
    right[...] = jnp.concatenate(
        [y1, y2, y1, y2, y3, y1, one8, one8, one8, n1, n2, n3], 0
    ).astype(BF16)
    eye = (
        lax.broadcasted_iota(jnp.int32, (128, 128), 0)
        == lax.broadcasted_iota(jnp.int32, (128, 128), 1)
    )
    held = []

    def apply(at, side, first, second):
        here = 2048 * piece + at
        v0 = vectors[:, here : here + 128]
        v1 = vectors[:, here + 128 : here + 256]
        out[:, at : at + 128] = mxu(v0, first, NN) + mxu(v1, side, NT)
        out[:, at + 128 : at + 256] = mxu(v0, side, NN) + mxu(v1, second, NN)

    for g in range(8 + DEPTH):
        if g < 8:
            at = 256 * g

            def block(a, b):
                square = mxu(left_t[at + a : at + a + 128, :], right[:, at + b : at + b + 128], NN)
                square = jnp.maximum(square, 1e-30)
                value = jnp.exp2(-(square * lax.rsqrt(square)))
                if a == b:
                    value = jnp.where(eye, NUGGET_DIAG, value)
                return value.astype(BF16)

            held.append((at, block(0, 128), block(0, 0), block(128, 128)))
        if g >= DEPTH:
            apply(*held[g - DEPTH])


NEAR_SCRATCH = [
    VMEM((8, 2048), F32),
    VMEM((2048, 96), BF16),
    VMEM((96, 2048), BF16),
]


def second_kernel(after, device, transfer, own_out, sib_out, quad_out, slab):
    dev = device[0]
    pick_rows(
        transfer.at[:, :, pl.ds(256, 252)], transfer_pick(dev, range(1, 7), 256, 252), slab
    )
    rows = [picked(slab, n) for n in range(16)]
    for n in range(6):
        own_out[n] = rows[n]
        sib_out[n] = rows[8 + n]
    own_out[6] = rows[14]
    own_out[7] = rows[15]
    up = [rows[1].astype(BF16), rows[9].astype(BF16)]
    for n, (row, side) in enumerate([(0, 0), (8, 0), (6, 1), (7, 1)]):
        quad_out[n] = mxu(rows[row].astype(BF16), up[side], NN)
    quad_out[4] = rows[6]
    quad_out[5] = rows[7]


def second_pick(after, device, transfer):
    return pl.pallas_call(
        second_kernel,
        out_shape=[
            jax.ShapeDtypeStruct((8, 64, 64), F32),
            jax.ShapeDtypeStruct((6, 64, 64), F32),
            jax.ShapeDtypeStruct((6, 64, 64), F32),
        ],
        in_specs=[IN_VMEM, IN_SMEM, IN_VMEM],
        out_specs=[IN_VMEM] * 3,
        scratch_shapes=[VMEM((32 * 24, 128), F32)],
        compiler_params=params(WINDOW_MIB),
        cost_estimate=cost(1),
        name="second_pick",
    )(after, device, transfer)


def combine_kernel(quad, own, a, b, c, up_out, sib_out):
    blocks = [own[...], a[...], b[...], c[...]]
    terms = [field_term(x, quad[n]) for n, x in enumerate(blocks)]
    up_out[...] = (terms[0] + terms[1]) + (terms[2] + terms[3])
    sib_out[...] = field_term(b[...], quad[4]) + field_term(c[...], quad[5])


def combine(quad, own, a, b, c):
    return pl.pallas_call(
        combine_kernel,
        out_shape=[jax.ShapeDtypeStruct((64, 64), F32)] * 2,
        in_specs=[IN_VMEM] * 5,
        out_specs=[IN_VMEM] * 2,
        compiler_params=params(WINDOW_MIB),
        cost_estimate=cost(0.3),
        name="combine",
    )(quad, own, a, b, c)


def lift_kernel(after, device, own0, own, table, lift_out, slab):
    dev = device[0]
    row = lax.broadcasted_iota(jnp.int32, (16, 255), 0)
    col = lax.broadcasted_iota(jnp.int32, (16, 255), 1)
    want = 256 - (256 >> row) + (jnp.full_like(row, dev) >> (row + 1))
    pick_rows(table, jnp.where((col == want) & (row < 8), 1.0, 0.0).astype(BF16), slab)
    turned = []
    for level in range(8):
        pair = picked(slab, level)
        odd = (dev >> level) & 1
        turned.append(jnp.where(odd == 1, pair, pair.T).astype(BF16))
    steps = [own0[...].T] + [own[n].T.astype(BF16) for n in range(6)]
    lift_out[0] = turned[0].astype(F32)
    chain = steps[0]
    for level in range(1, 8):
        hi = chain.astype(BF16)
        lo = (chain - hi.astype(F32)).astype(BF16)
        if level < 7:
            chain = mxu(steps[level], hi, NN) + mxu(steps[level], lo, NN)
        last = mxu(turned[level], hi, NN) + mxu(turned[level], lo, NN)
        if level < 7:
            lift_out[level] = last
    hi = last.astype(BF16)
    lo = (last - hi.astype(F32)).astype(BF16)
    for n in range(2):
        e = own[6 + n].astype(BF16)
        lift_out[7 + n] = mxu(e, hi, NN) + mxu(e, lo, NN)


def lifts(after, device, own0, own, coupling):
    return pl.pallas_call(
        lift_kernel,
        out_shape=jax.ShapeDtypeStruct((9, 64, 64), F32),
        in_specs=[IN_VMEM, IN_SMEM, IN_VMEM, IN_VMEM, IN_VMEM],
        out_specs=IN_VMEM,
        scratch_shapes=[VMEM((32 * 24, 128), F32)],
        compiler_params=params(WINDOW_MIB),
        cost_estimate=cost(2),
        name="lifts",
    )(after, device, own0, own, coupling)


def near_kernel(piece, after, coords, vectors, near_out, square_x, left_t, right):
    near_field(piece, coords, vectors, near_out, square_x, left_t, right)


def near(piece, after, coords, vectors):
    return pl.pallas_call(
        functools.partial(near_kernel, piece),
        out_shape=jax.ShapeDtypeStruct((64, 2048), F32),
        in_specs=[IN_VMEM] * 3,
        out_specs=IN_VMEM,
        scratch_shapes=NEAR_SCRATCH,
        compiler_params=params(WINDOW_MIB),
        cost_estimate=cost(1.5),
        name="near",
    )(after, coords, vectors)


def shift_right():
    row = lax.broadcasted_iota(jnp.int32, (64, 128), 0)
    col = lax.broadcasted_iota(jnp.int32, (64, 128), 1)
    return jnp.where(col == row + 64, 1.0, 0.0).astype(BF16)


def pair_fields(coefs, couplings, shift):
    blank = jnp.zeros((64, 128), BF16)
    sides = [jnp.concatenate([mxu(c[...], shift, NN).astype(BF16), blank], 0) for c in couplings]
    parts = [split(c[...]) for c in coefs]
    terms = [(mxu(s, z, NN), mxu(s, z, NT)) for s, z in zip(parts, sides)]
    return [fold(a + b) for a, b in terms]


def with_fields(state, fields):
    return jnp.concatenate([state[:64] + jnp.concatenate(fields, 1), state[64:]], 0)


def descend(state, quad):
    return fold(mxu(split(state), quad, NT))


def upper_kernel(after, coupling, levels, quads, state_out):
    shift = shift_right()

    where = [(level, pair) for level in range(6, 2, -1) for pair in range((64 >> level))]
    found = pair_fields(
        [levels.at[:, pl.ds(LEVEL_AT[level] - 4096 + 128 * pair, 128)] for level, pair in where],
        [coupling.at[32 - (32 >> (level - 2)) + pair] for level, pair in where],
        shift,
    )
    found = dict(zip(where, found))

    def field(level, pair):
        return found[level, pair]

    unit = jnp.where(
        lax.broadcasted_iota(jnp.int32, (64, 64), 0)
        == lax.broadcasted_iota(jnp.int32, (64, 64), 1),
        1.0,
        0.0,
    ).astype(BF16)
    state = jnp.concatenate([field(6, 0), mxu(unit, quads[7, :128, :64], NT)], 0)
    for level in range(5, 2, -1):
        below = []
        for q in range((128 >> level) // 4):
            s = descend(state[:, 128 * q : 128 * q + 128], quads[NODE_AT[level] // 4 - 56 + q])
            below.append(with_fields(s, [field(level, 2 * q), field(level, 2 * q + 1)]))
        state = jnp.concatenate(below, 1)
    state_out[...] = state


def upper(after, coupling, levels, quads):
    return pl.pallas_call(
        upper_kernel,
        out_shape=jax.ShapeDtypeStruct((128, 1024), F32),
        in_specs=[IN_VMEM] * 4,
        out_specs=IN_VMEM,
        compiler_params=params(WINDOW_MIB),
        cost_estimate=cost(1.5),
        name="upper",
    )(after, coupling, levels, quads)


def lower_kernel(piece, after, state3, near_in, coupling, levels, quads, pairs, base_out, top_out):
    shift = shift_right()
    mine = range(4 * piece, 4 * piece + 4)
    fields = pair_fields(
        [levels.at[:, pl.ds(128 * p, 128)] for p in mine],
        [coupling.at[p] for p in mine],
        shift,
    )
    state = state3[:, 256 * piece : 256 * piece + 256]
    state = jnp.concatenate(
        [
            with_fields(
                descend(state[:, 128 * q : 128 * q + 128], quads[48 + 2 * piece + q]),
                fields[2 * q : 2 * q + 2],
            )
            for q in range(2)
        ],
        1,
    )
    state = jnp.concatenate(
        [descend(state[:, 128 * q : 128 * q + 128], quads[32 + 4 * piece + q]) for q in range(4)], 1
    )
    leaves = []
    for q in range(8 + DEPTH):
        if q < 8:
            leaves.append(descend(state[:, 128 * q : 128 * q + 128], quads[8 * piece + q]))
        if q >= DEPTH:
            for u in range(2):
                pair = 2 * (q - DEPTH) + u
                at = 128 * pair
                t = descend(
                    leaves[q - DEPTH][:, 128 * u : 128 * u + 128], pairs[16 * piece + pair]
                )
                base_out[:, at : at + 128] = t[:64] + near_in[:, at : at + 128]
                top_out[:, at : at + 128] = split(t[64:])


def lower_piece(piece, after, state3, near_in, coupling, levels, quads, pairs):
    return pl.pallas_call(
        functools.partial(lower_kernel, piece),
        out_shape=[
            jax.ShapeDtypeStruct((64, 2048), F32),
            jax.ShapeDtypeStruct((128, 2048), BF16),
        ],
        in_specs=[IN_VMEM] * 7,
        out_specs=[IN_VMEM] * 2,
        compiler_params=params(WINDOW_MIB),
        cost_estimate=cost(1.5),
        name="lower",
    )(after, state3, near_in, coupling, levels, quads, pairs)


def field_term(partner, lift):
    hi = lift.astype(BF16)
    lo = (lift - hi.astype(F32)).astype(BF16)
    p = split(partner)
    return fold(mxu(p, hi, NN)) + mxu(p[:64], lo, NN)


def partial_kernel(after, lift, *refs):
    terms = [field_term(refs[height][...], lift[height]) for height in range(6)]
    refs[6][...] = sum(terms[1:], terms[0])


def partial_field(after, lift, partners):
    return pl.pallas_call(
        partial_kernel,
        out_shape=jax.ShapeDtypeStruct((64, 64), F32),
        in_specs=[IN_VMEM] * 8,
        out_specs=IN_VMEM,
        compiler_params=params(WINDOW_MIB),
        cost_estimate=cost(0.5),
        name="partial_field",
    )(after, lift, *partners)


def final_kernel(lift, partial, *refs):
    bases = refs[3:7]
    tops = refs[7:11]
    out_h, out, sems = refs[11:]
    terms = [field_term(refs[n][...], lift[6 + n]) for n in range(3)]
    g = (partial[...] + terms[0]) + (terms[1] + terms[2])
    hi = g.astype(BF16)
    lo = (g - hi.astype(F32)).astype(BF16)
    g = jnp.concatenate(
        [jnp.concatenate([hi, hi], 1), jnp.concatenate([lo, jnp.zeros_like(lo)], 1)], 0
    )
    copies = []
    for piece in range(4):
        for q in range(8):
            at = 256 * q
            out[:, 2048 * piece + at : 2048 * piece + at + 256] = (
                fold(mxu(g, tops[piece][:, at : at + 256], NN)) + bases[piece][:, at : at + 256]
            )
            if q % 4 == 3:
                part = pl.ds(2048 * piece + at - 768, 1024)
                copies.append(
                    pltpu.make_async_copy(
                        out.at[:, part], out_h.at[:, part], sems.at[len(copies)]
                    )
                )
                copies[-1].start()
    for copy in copies:
        copy.wait()


def final(lift, partial, partners, bases, tops):
    return pl.pallas_call(
        final_kernel,
        out_shape=jax.ShapeDtypeStruct((64, 8192), F32),
        in_specs=[IN_VMEM] * 13,
        out_specs=IN_HBM,
        scratch_shapes=[VMEM((64, 8192), F32), pltpu.SemaphoreType.DMA((8,))],
        compiler_params=params(16),
        cost_estimate=cost(2),
        name="final",
    )(lift, partial, *partners, *bases, *tops)


def climb_kernel(row, own, sib, mine, other, out):
    a, b = (own[...], sib[...]) if row is None else (own[row], sib[row])
    out[...] = fold(
        mxu(split(mine[...]), a.astype(BF16), NN) + mxu(split(other[...]), b.astype(BF16), NN)
    )


def climb(row, own, sib, mine, other):
    return pl.pallas_call(
        functools.partial(climb_kernel, row),
        out_shape=jax.ShapeDtypeStruct((64, 64), F32),
        in_specs=[IN_VMEM] * 4,
        out_specs=IN_VMEM,
        compiler_params=params(WINDOW_MIB),
        cost_estimate=cost(0.2),
        name="climb",
    )(own, sib, mine, other)


def exchanged(value, mask):
    devices = lax.axis_size(AXES)
    return lax.ppermute(value, AXES, [(s, s ^ mask) for s in range(devices)])


def on_device(coords, vectors, bases, transfer, coupling, top_transfer, top_coupling):
    vectors = vectors.T
    device = lax.axis_index(AXES).astype(jnp.int32).reshape(1)
    climbing, own0, sib0, levels, quads_top, pairs, quads = upward(
        device,
        bases.transpose(1, 2, 0),
        vectors,
        transfer[0].transpose(1, 2, 0),
        top_transfer.transpose(1, 2, 0),
    )
    top_transfer = top_transfer.transpose(1, 2, 0)
    table2 = top_coupling.transpose(1, 2, 0)
    coupling = coupling[0]
    lows = []

    def lower_with(after, piece, near_in):
        lows.append(lower_piece(piece, after, state, near_in, coupling, levels, quads, pairs))

    fields = [exchanged(climbing, 1)]
    near0 = near(0, climbing, coords, vectors)
    climbing = climb(None, own0, sib0, climbing, fields[0])
    start = climbing
    owns, sibs, quad = second_pick(start, device, top_transfer)
    ring = [exchanged(start, mask) for mask in (2, 4, 6)]
    near1 = near(1, start, coords, vectors)
    climbing, sibling = combine(quad, start, *ring)
    fields += [ring[0], sibling]
    for height, mask in ((3, 8), (4, 16), (5, 48)):
        start = climbing
        fields.append(exchanged(start, mask))
        if height == 3:
            lift = lifts(start, device, own0, owns, table2)
        elif height == 4:
            state = upper(start, coupling, levels, quads_top)
            near2 = near(2, start, coords, vectors)
        else:
            near3 = near(3, start, coords, vectors)
            lower_with(start, 0, near0)
        climbing = climb(height - 1, owns, sibs, start, fields[-1])
    ring = [exchanged(climbing, mask) for mask in (64, 128, 192)]
    lower_with(climbing, 1, near1)
    lower_with(climbing, 2, near2)
    lower_with(climbing, 3, near3)
    partial = partial_field(climbing, lift, fields)
    result = final(lift, partial, ring, [low[0] for low in lows], [low[1] for low in lows])
    return result.T


def solution(mesh):
    both = ("leaf", "sub")
    return jax.shard_map(
        on_device,
        mesh=mesh,
        in_specs=(
            P(None, both),
            P(both, None),
            P(both, None, None),
            P(both, None, None, None),
            P(both, None, None, None),
            P(),
            P(),
        ),
        out_specs=P(both, None),
        check_vma=False,
    )
```

```python
import functools

import jax
import jax.numpy as jnp
from jax import lax
from jax.experimental import pallas as pl
from jax.experimental.pallas import tpu as pltpu
from jax.sharding import PartitionSpec as P

F32 = jnp.float32
BF16 = jnp.bfloat16
VMEM = pltpu.VMEM
AXES = ("leaf", "sub")

STEP = 136
NN = (((1,), (0,)), ((), ()))
NT = (((1,), (1,)), ((), ()))
LEVEL_AT = (None, 0, 4096, 6144, 7168, 7680, 7936)
NODE_AT = (0, 128, 192, 224, 240, 248, 252)
NUGGET_DIAG = 1.5
CHORD = 2.0 * 1.4426950408889634


def mxu(a, b, dims):
    return lax.dot_general(a, b, dims, preferred_element_type=F32)


def split(c):
    hi = c.astype(BF16)
    lo = (c - hi.astype(F32)).astype(BF16)
    return jnp.concatenate([hi, lo], 0)


def fold(t):
    half = t.shape[0] // 2
    return t[:half] + t[half:]


def half_mask():
    return lax.broadcasted_iota(jnp.int32, (32, 128), 1) < 64


def spread(src, width, lane0, slab, rows):
    for i in rows:
        w = jnp.concatenate([src[i, :, lane0 : lane0 + width], src[i + 32, :, lane0 : lane0 + width]], 0)
        if width < 128:
            w = jnp.concatenate([w, jnp.zeros((128, 128 - width), BF16)], 1)
        slab[pl.ds(i * STEP, 128), :] = w.T.astype(F32)


def box_matrix(slab, box, right, low):
    x = slab[pl.ds(box, 32, stride=STEP), :]
    y = pltpu.roll(x, 64, 1)
    if right:
        return jnp.concatenate([jnp.where(low, 0.0, y), jnp.where(low, 0.0, x)], 0)
    return jnp.concatenate([jnp.where(low, x, 0.0), jnp.where(low, y, 0.0)], 0)


def up_kernel(
    device, bases_h, vectors_h, transfer_h, top_transfer_h,
    own_out, own0_out, sib0_out, levels, quads_top, pairs_h, quads_h,
    bases, vectors, transfer, slab0, slab1, slab2, leaf_coef, level1, pairs, quads, table0, picks, sems, out_sems,
):
    loads = []
    for k in range(4):
        part = pl.ds(16 * (k // 2) + 32 * (k % 2), 16)
        loads.append(pltpu.make_async_copy(bases_h.at[part], bases.at[part], sems.at[k]))
    loads.append(pltpu.make_async_copy(vectors_h, vectors, sems.at[4]))
    loads.append(pltpu.make_async_copy(transfer_h, transfer, sems.at[5]))
    lane0 = pl.multiple_of(128 * (device[0] >> 7), 128)
    loads.append(
        pltpu.make_async_copy(top_transfer_h.at[:, :, pl.ds(lane0, 128)], table0, sems.at[6])
    )
    for copy in loads:
        copy.start()
    stores = []

    def store(src, dst):
        copy = pltpu.make_async_copy(src, dst, out_sems.at[len(stores)])
        copy.start()
        stores.append(copy)

    low = half_mask()
    for k in range(2):
        loads[2 * k].wait()
        loads[2 * k + 1].wait()
        spread(bases, 128, 0, slab0, range(16 * k, 16 * k + 16))
    loads[4].wait()
    held = []
    for j in range(64 + DEPTH):
        if j == 16:
            loads[5].wait()
        if j < 64:
            pair = jnp.concatenate(
                [box_matrix(slab0, 2 * j, False, low), box_matrix(slab0, 2 * j + 1, True, low)], 0
            ).astype(BF16)
            pairs[j] = pair
            held.append(pair)
        if 16 <= j < 48:
            spread(transfer, 128, 0, slab1, [j - 16])
        if j >= DEPTH:
            at = 128 * (j - DEPTH)
            leaf_coef[:, at : at + 128] = mxu(vectors[:, at : at + 128], held[j - DEPTH], NN)
    store(pairs, pairs_h)
    steps = [(level, q) for level in range(6) for q in range((128 >> level) // 4)]
    held = []
    for k in range(len(steps) + UP_DEPTH):
        if k < 16:
            spread(transfer, 126, 128, slab2, [2 * k, 2 * k + 1])
        if k == 51:
            loads[6].wait()
            first_pick = transfer_pick(device[0], [0], lane0, 128)
        if 51 <= k < 67:
            pick_row(table0, first_pick, picks, k - 51)
        if k < len(steps):
            level, q = steps[k]
            first = NODE_AT[level] + 4 * q
            slab = slab1 if first < 128 else slab2
            quad = jnp.concatenate(
                [box_matrix(slab, (first + u) % 128, u >= 2, low) for u in range(4)], 0
            ).astype(BF16)
            if level < 3:
                quads[first // 4] = quad
                if q == (32 >> level) - 1:
                    part = pl.ds(NODE_AT[level] // 4, 32 >> level)
                    store(quads.at[part], quads_h.at[part])
            else:
                quads_top[first // 4 - 56] = quad
            held.append(quad)
        if k >= UP_DEPTH:
            level, q = steps[k - UP_DEPTH]
            if level == 0:
                coef = leaf_coef[:, 256 * q : 256 * q + 256]
            elif level == 1:
                coef = level1[:, 256 * q : 256 * q + 256]
            else:
                at = LEVEL_AT[level] - 4096 + 256 * q
                coef = levels[:, at : at + 256]
            coef = fold(mxu(split(coef), held[k - UP_DEPTH], NN))
            if level == 0:
                level1[:, 128 * q : 128 * q + 128] = coef
            else:
                at = LEVEL_AT[level + 1] - 4096 + 128 * q
                levels[:, at : at + 128] = coef
    last = jnp.concatenate(
        [box_matrix(slab2, 124, False, low), box_matrix(slab2, 125, False, low)], 0
    ).astype(BF16)
    quads_top[7, :128, :] = last
    quads_top[7, 128:, :] = jnp.zeros((128, 128), BF16)
    at = LEVEL_AT[6] - 4096
    own_out[...] = fold(mxu(split(levels[:, at : at + 128]), last, NN))[:, :64]
    own0_out[...] = picked(picks, 0)
    sib0_out[...] = picked(picks, 8)
    for copy in stores:
        copy.wait()


def params(mib):
    return pltpu.CompilerParams(vmem_limit_bytes=mib * 2**20)


def cost(us):
    return pl.CostEstimate(flops=int(us * 10**9), bytes_accessed=2**16, transcendentals=0)


UP_MIB = 52
WINDOW_MIB = 12
UP_DEPTH = 8
DEPTH = 3
IN_VMEM = pl.BlockSpec(memory_space=VMEM)
IN_HBM = pl.BlockSpec(memory_space=pl.ANY)
IN_SMEM = pl.BlockSpec(memory_space=pltpu.SMEM)


def upward(device, bases, vectors, transfer, top_transfer):
    return pl.pallas_call(
        up_kernel,
        out_shape=[
            jax.ShapeDtypeStruct((64, 64), F32),
            jax.ShapeDtypeStruct((64, 64), F32),
            jax.ShapeDtypeStruct((64, 64), F32),
            jax.ShapeDtypeStruct((64, 3968), F32),
            jax.ShapeDtypeStruct((8, 256, 128), BF16),
            jax.ShapeDtypeStruct((64, 128, 128), BF16),
            jax.ShapeDtypeStruct((56, 256, 128), BF16),
        ],
        in_specs=[IN_SMEM] + [IN_HBM] * 4,
        out_specs=[IN_VMEM] * 5 + [IN_HBM] * 2,
        scratch_shapes=[
            VMEM((64, 64, 128), BF16),
            VMEM((64, 8192), BF16),
            VMEM((64, 64, 254), BF16),
            VMEM((32 * STEP, 128), F32),
            VMEM((32 * STEP, 128), F32),
            VMEM((32 * STEP, 128), F32),
            VMEM((64, 8192), F32),
            VMEM((64, 4096), F32),
            VMEM((64, 128, 128), BF16),
            VMEM((56, 256, 128), BF16),
            VMEM((64, 64, 128), BF16),
            VMEM((32 * 24, 128), F32),
            pltpu.SemaphoreType.DMA((7,)),
            pltpu.SemaphoreType.DMA((4,)),
        ],
        compiler_params=params(UP_MIB),
        cost_estimate=cost(8),
        name="upward",
    )(device, bases, vectors, transfer, top_transfer)


def pick_row(table, pick, slab, i):
    rows = jnp.concatenate(
        [table[2 * i], table[2 * i + 32], table[2 * i + 1], table[2 * i + 33]], 0
    )
    out = mxu(pick, rows, NT)
    slab[pl.ds(48 * i, 16), :] = out[:, :128]
    slab[pl.ds(48 * i + 24, 16), :] = out[:, 128:]


def pick_rows(table, pick, slab):
    for i in range(16):
        pick_row(table, pick, slab, i)


def picked(slab, row):
    x = slab[pl.ds(row, 32, stride=24), :]
    return jnp.concatenate([x, pltpu.roll(x, 64, 1)], 0)[:, :64]


def transfer_pick(dev, heights, lane0, width):
    row = lax.broadcasted_iota(jnp.int32, (16, width), 0)
    col = lax.broadcasted_iota(jnp.int32, (16, width), 1)
    hit = jnp.zeros((16, width), jnp.bool_)
    for n, height in enumerate(heights):
        box = 512 - (512 >> height) + (dev >> height) - lane0
        hit = hit | ((row == n) & (col == box))
        hit = hit | ((row == n + 8) & (col == (box ^ 1)))
        if height in (1, 6):
            extra = 6 if height == 1 else 14
            hit = hit | ((row == extra) & (col == (box ^ 2)))
            hit = hit | ((row == extra + 1) & (col == (box ^ 3)))
    return jnp.where(hit, 1.0, 0.0).astype(BF16)


def thirds(x):
    a = x.astype(BF16).astype(F32)
    b = (x - a).astype(BF16).astype(F32)
    return a, b, x - a - b


def near_field(piece, coords, vectors, out, square_x, left_t, right):
    square_x[0:3, :] = coords[:, 2048 * piece : 2048 * piece + 2048] * CHORD
    square_x[3:8, :] = jnp.zeros((5, 2048), F32)
    x = square_x[...]
    one8 = jnp.where(lax.broadcasted_iota(jnp.int32, (8, 2048), 0) == 0, 1.0, 0.0)
    x1, x2, x3 = thirds(x)
    n1, n2, n3 = thirds(jnp.sum(x * x, axis=0, keepdims=True) * one8)
    left = jnp.concatenate([x1, x1, x2, x2, x1, x3, n1, n2, n3, one8, one8, one8], 0)
    left_t[...] = left.astype(BF16).T
    y1, y2, y3 = -2 * x1, -2 * x2, -2 * x3
    right[...] = jnp.concatenate(
        [y1, y2, y1, y2, y3, y1, one8, one8, one8, n1, n2, n3], 0
    ).astype(BF16)
    eye = (
        lax.broadcasted_iota(jnp.int32, (128, 128), 0)
        == lax.broadcasted_iota(jnp.int32, (128, 128), 1)
    )
    held = []

    def apply(at, side, first, second):
        here = 2048 * piece + at
        v0 = vectors[:, here : here + 128]
        v1 = vectors[:, here + 128 : here + 256]
        out[:, at : at + 128] = mxu(v0, first, NN) + mxu(v1, side, NT)
        out[:, at + 128 : at + 256] = mxu(v0, side, NN) + mxu(v1, second, NN)

    for g in range(8 + DEPTH):
        if g < 8:
            at = 256 * g

            def block(a, b):
                square = mxu(left_t[at + a : at + a + 128, :], right[:, at + b : at + b + 128], NN)
                square = jnp.maximum(square, 1e-30)
                value = jnp.exp2(-(square * lax.rsqrt(square)))
                if a == b:
                    value = jnp.where(eye, NUGGET_DIAG, value)
                return value.astype(BF16)

            held.append((at, block(0, 128), block(0, 0), block(128, 128)))
        if g >= DEPTH:
            apply(*held[g - DEPTH])


NEAR_SCRATCH = [
    VMEM((8, 2048), F32),
    VMEM((2048, 96), BF16),
    VMEM((96, 2048), BF16),
]


def second_kernel(after, device, transfer, own_out, sib_out, quad_out, slab):
    dev = device[0]
    pick_rows(
        transfer.at[:, :, pl.ds(256, 252)], transfer_pick(dev, range(1, 7), 256, 252), slab
    )
    rows = [picked(slab, n) for n in range(16)]
    for n in range(6):
        own_out[n] = rows[n]
        sib_out[n] = rows[8 + n]
    own_out[6] = rows[14]
    own_out[7] = rows[15]
    up = [rows[1].astype(BF16), rows[9].astype(BF16)]
    for n, (row, side) in enumerate([(0, 0), (8, 0), (6, 1), (7, 1)]):
        quad_out[n] = mxu(rows[row].astype(BF16), up[side], NN)
    quad_out[4] = rows[6]
    quad_out[5] = rows[7]


def second_pick(after, device, transfer):
    return pl.pallas_call(
        second_kernel,
        out_shape=[
            jax.ShapeDtypeStruct((8, 64, 64), F32),
            jax.ShapeDtypeStruct((6, 64, 64), F32),
            jax.ShapeDtypeStruct((6, 64, 64), F32),
        ],
        in_specs=[IN_VMEM, IN_SMEM, IN_VMEM],
        out_specs=[IN_VMEM] * 3,
        scratch_shapes=[VMEM((32 * 24, 128), F32)],
        compiler_params=params(WINDOW_MIB),
        cost_estimate=cost(1),
        name="second_pick",
    )(after, device, transfer)


def combine_kernel(quad, own, a, b, c, up_out, sib_out):
    blocks = [own[...], a[...], b[...], c[...]]
    terms = [field_term(x, quad[n]) for n, x in enumerate(blocks)]
    up_out[...] = (terms[0] + terms[1]) + (terms[2] + terms[3])
    sib_out[...] = field_term(b[...], quad[4]) + field_term(c[...], quad[5])


def combine(quad, own, a, b, c):
    return pl.pallas_call(
        combine_kernel,
        out_shape=[jax.ShapeDtypeStruct((64, 64), F32)] * 2,
        in_specs=[IN_VMEM] * 5,
        out_specs=[IN_VMEM] * 2,
        compiler_params=params(WINDOW_MIB),
        cost_estimate=cost(0.3),
        name="combine",
    )(quad, own, a, b, c)


def lift_kernel(after, device, own0, own, table, lift_out, slab):
    dev = device[0]
    row = lax.broadcasted_iota(jnp.int32, (16, 255), 0)
    col = lax.broadcasted_iota(jnp.int32, (16, 255), 1)
    want = 256 - (256 >> row) + (jnp.full_like(row, dev) >> (row + 1))
    pick_rows(table, jnp.where((col == want) & (row < 8), 1.0, 0.0).astype(BF16), slab)
    turned = []
    for level in range(8):
        pair = picked(slab, level)
        odd = (dev >> level) & 1
        turned.append(jnp.where(odd == 1, pair, pair.T).astype(BF16))
    steps = [own0[...].T] + [own[n].T.astype(BF16) for n in range(6)]
    lift_out[0] = turned[0].astype(F32)
    chain = steps[0]
    for level in range(1, 8):
        hi = chain.astype(BF16)
        lo = (chain - hi.astype(F32)).astype(BF16)
        if level < 7:
            chain = mxu(steps[level], hi, NN) + mxu(steps[level], lo, NN)
        last = mxu(turned[level], hi, NN) + mxu(turned[level], lo, NN)
        if level < 7:
            lift_out[level] = last
    hi = last.astype(BF16)
    lo = (last - hi.astype(F32)).astype(BF16)
    for n in range(2):
        e = own[6 + n].astype(BF16)
        lift_out[7 + n] = mxu(e, hi, NN) + mxu(e, lo, NN)


def lifts(after, device, own0, own, coupling):
    return pl.pallas_call(
        lift_kernel,
        out_shape=jax.ShapeDtypeStruct((9, 64, 64), F32),
        in_specs=[IN_VMEM, IN_SMEM, IN_VMEM, IN_VMEM, IN_VMEM],
        out_specs=IN_VMEM,
        scratch_shapes=[VMEM((32 * 24, 128), F32)],
        compiler_params=params(WINDOW_MIB),
        cost_estimate=cost(2),
        name="lifts",
    )(after, device, own0, own, coupling)


def near_kernel(piece, after, coords, vectors, near_out, square_x, left_t, right):
    near_field(piece, coords, vectors, near_out, square_x, left_t, right)


def near(piece, after, coords, vectors):
    return pl.pallas_call(
        functools.partial(near_kernel, piece),
        out_shape=jax.ShapeDtypeStruct((64, 2048), F32),
        in_specs=[IN_VMEM] * 3,
        out_specs=IN_VMEM,
        scratch_shapes=NEAR_SCRATCH,
        compiler_params=params(WINDOW_MIB),
        cost_estimate=cost(1.5),
        name="near",
    )(after, coords, vectors)


def shift_right():
    row = lax.broadcasted_iota(jnp.int32, (64, 128), 0)
    col = lax.broadcasted_iota(jnp.int32, (64, 128), 1)
    return jnp.where(col == row + 64, 1.0, 0.0).astype(BF16)


def pair_fields(coefs, couplings, shift):
    blank = jnp.zeros((64, 128), BF16)
    sides = [jnp.concatenate([mxu(c[...], shift, NN).astype(BF16), blank], 0) for c in couplings]
    parts = [split(c[...]) for c in coefs]
    terms = [(mxu(s, z, NN), mxu(s, z, NT)) for s, z in zip(parts, sides)]
    return [fold(a + b) for a, b in terms]


def with_fields(state, fields):
    return jnp.concatenate([state[:64] + jnp.concatenate(fields, 1), state[64:]], 0)


def descend(state, quad):
    return fold(mxu(split(state), quad, NT))


def upper_kernel(after, coupling, levels, quads, state_out):
    shift = shift_right()

    where = [(level, pair) for level in range(6, 2, -1) for pair in range((64 >> level))]
    found = pair_fields(
        [levels.at[:, pl.ds(LEVEL_AT[level] - 4096 + 128 * pair, 128)] for level, pair in where],
        [coupling.at[32 - (32 >> (level - 2)) + pair] for level, pair in where],
        shift,
    )
    found = dict(zip(where, found))

    def field(level, pair):
        return found[level, pair]

    unit = jnp.where(
        lax.broadcasted_iota(jnp.int32, (64, 64), 0)
        == lax.broadcasted_iota(jnp.int32, (64, 64), 1),
        1.0,
        0.0,
    ).astype(BF16)
    state = jnp.concatenate([field(6, 0), mxu(unit, quads[7, :128, :64], NT)], 0)
    for level in range(5, 2, -1):
        below = []
        for q in range((128 >> level) // 4):
            s = descend(state[:, 128 * q : 128 * q + 128], quads[NODE_AT[level] // 4 - 56 + q])
            below.append(with_fields(s, [field(level, 2 * q), field(level, 2 * q + 1)]))
        state = jnp.concatenate(below, 1)
    state_out[...] = state


def upper(after, coupling, levels, quads):
    return pl.pallas_call(
        upper_kernel,
        out_shape=jax.ShapeDtypeStruct((128, 1024), F32),
        in_specs=[IN_VMEM] * 4,
        out_specs=IN_VMEM,
        compiler_params=params(WINDOW_MIB),
        cost_estimate=cost(1.5),
        name="upper",
    )(after, coupling, levels, quads)


def lower_kernel(piece, after, state3, near_in, coupling, levels, quads, pairs, base_out, top_out):
    shift = shift_right()
    mine = range(4 * piece, 4 * piece + 4)
    fields = pair_fields(
        [levels.at[:, pl.ds(128 * p, 128)] for p in mine],
        [coupling.at[p] for p in mine],
        shift,
    )
    state = state3[:, 256 * piece : 256 * piece + 256]
    state = jnp.concatenate(
        [
            with_fields(
                descend(state[:, 128 * q : 128 * q + 128], quads[48 + 2 * piece + q]),
                fields[2 * q : 2 * q + 2],
            )
            for q in range(2)
        ],
        1,
    )
    state = jnp.concatenate(
        [descend(state[:, 128 * q : 128 * q + 128], quads[32 + 4 * piece + q]) for q in range(4)], 1
    )
    leaves = []
    for q in range(8 + DEPTH):
        if q < 8:
            leaves.append(descend(state[:, 128 * q : 128 * q + 128], quads[8 * piece + q]))
        if q >= DEPTH:
            for u in range(2):
                pair = 2 * (q - DEPTH) + u
                at = 128 * pair
                t = descend(
                    leaves[q - DEPTH][:, 128 * u : 128 * u + 128], pairs[16 * piece + pair]
                )
                base_out[:, at : at + 128] = t[:64] + near_in[:, at : at + 128]
                top_out[:, at : at + 128] = split(t[64:])


def lower_piece(piece, after, state3, near_in, coupling, levels, quads, pairs):
    return pl.pallas_call(
        functools.partial(lower_kernel, piece),
        out_shape=[
            jax.ShapeDtypeStruct((64, 2048), F32),
            jax.ShapeDtypeStruct((128, 2048), BF16),
        ],
        in_specs=[IN_VMEM] * 7,
        out_specs=[IN_VMEM] * 2,
        compiler_params=params(WINDOW_MIB),
        cost_estimate=cost(1.5),
        name="lower",
    )(after, state3, near_in, coupling, levels, quads, pairs)


def field_term(partner, lift):
    hi = lift.astype(BF16)
    lo = (lift - hi.astype(F32)).astype(BF16)
    p = split(partner)
    return fold(mxu(p, hi, NN)) + mxu(p[:64], lo, NN)


def partial_kernel(after, lift, *refs):
    terms = [field_term(refs[height][...], lift[height]) for height in range(6)]
    refs[6][...] = sum(terms[1:], terms[0])


def partial_field(after, lift, partners):
    return pl.pallas_call(
        partial_kernel,
        out_shape=jax.ShapeDtypeStruct((64, 64), F32),
        in_specs=[IN_VMEM] * 8,
        out_specs=IN_VMEM,
        compiler_params=params(WINDOW_MIB),
        cost_estimate=cost(0.5),
        name="partial_field",
    )(after, lift, *partners)


def final_kernel(lift, partial, *refs):
    bases = refs[3:7]
    tops = refs[7:11]
    out_h, out, sems = refs[11:]
    terms = [field_term(refs[n][...], lift[6 + n]) for n in range(3)]
    g = (partial[...] + terms[0]) + (terms[1] + terms[2])
    hi = g.astype(BF16)
    lo = (g - hi.astype(F32)).astype(BF16)
    g = jnp.concatenate(
        [jnp.concatenate([hi, hi], 1), jnp.concatenate([lo, jnp.zeros_like(lo)], 1)], 0
    )
    copies = []
    for piece in range(4):
        for q in range(8):
            at = 256 * q
            out[:, 2048 * piece + at : 2048 * piece + at + 256] = (
                fold(mxu(g, tops[piece][:, at : at + 256], NN)) + bases[piece][:, at : at + 256]
            )
            if q % 4 == 3:
                part = pl.ds(2048 * piece + at - 768, 1024)
                copies.append(
                    pltpu.make_async_copy(
                        out.at[:, part], out_h.at[:, part], sems.at[len(copies)]
                    )
                )
                copies[-1].start()
    for copy in copies:
        copy.wait()


def final(lift, partial, partners, bases, tops):
    return pl.pallas_call(
        final_kernel,
        out_shape=jax.ShapeDtypeStruct((64, 8192), F32),
        in_specs=[IN_VMEM] * 13,
        out_specs=IN_HBM,
        scratch_shapes=[VMEM((64, 8192), F32), pltpu.SemaphoreType.DMA((8,))],
        compiler_params=params(16),
        cost_estimate=cost(2),
        name="final",
    )(lift, partial, *partners, *bases, *tops)


def climb_kernel(row, own, sib, mine, other, out):
    a, b = (own[...], sib[...]) if row is None else (own[row], sib[row])
    out[...] = fold(
        mxu(split(mine[...]), a.astype(BF16), NN) + mxu(split(other[...]), b.astype(BF16), NN)
    )


def climb(row, own, sib, mine, other):
    return pl.pallas_call(
        functools.partial(climb_kernel, row),
        out_shape=jax.ShapeDtypeStruct((64, 64), F32),
        in_specs=[IN_VMEM] * 4,
        out_specs=IN_VMEM,
        compiler_params=params(WINDOW_MIB),
        cost_estimate=cost(0.2),
        name="climb",
    )(own, sib, mine, other)


def exchanged(value, mask):
    devices = lax.axis_size(AXES)
    return lax.ppermute(value, AXES, [(s, s ^ mask) for s in range(devices)])


def on_device(coords, vectors, bases, transfer, coupling, top_transfer, top_coupling):
    vectors = vectors.T
    device = lax.axis_index(AXES).astype(jnp.int32).reshape(1)
    climbing, own0, sib0, levels, quads_top, pairs, quads = upward(
        device,
        bases.transpose(1, 2, 0),
        vectors,
        transfer[0].transpose(1, 2, 0),
        top_transfer.transpose(1, 2, 0),
    )
    top_transfer = top_transfer.transpose(1, 2, 0)
    table2 = top_coupling.transpose(1, 2, 0)
    coupling = coupling[0]
    lows = []

    def lower_with(after, piece, near_in):
        lows.append(lower_piece(piece, after, state, near_in, coupling, levels, quads, pairs))

    fields = [exchanged(climbing, 1)]
    near0 = near(0, climbing, coords, vectors)
    climbing = climb(None, own0, sib0, climbing, fields[0])
    start = climbing
    owns, sibs, quad = second_pick(start, device, top_transfer)
    ring = [exchanged(start, mask) for mask in (2, 4, 6)]
    near1 = near(1, start, coords, vectors)
    climbing, sibling = combine(quad, start, *ring)
    fields += [ring[0], sibling]
    for height, mask in ((3, 8), (4, 16), (5, 48)):
        start = climbing
        fields.append(exchanged(start, mask))
        if height == 3:
            lift = lifts(start, device, own0, owns, table2)
        elif height == 4:
            state = upper(start, coupling, levels, quads_top)
            near2 = near(2, start, coords, vectors)
        else:
            near3 = near(3, start, coords, vectors)
            lower_with(start, 0, near0)
        climbing = climb(height - 1, owns, sibs, start, fields[-1])
    ring = [exchanged(climbing, mask) for mask in (64, 128, 192)]
    lower_with(climbing, 1, near1)
    lower_with(climbing, 2, near2)
    lower_with(climbing, 3, near3)
    partial = partial_field(climbing, lift, fields)
    result = final(lift, partial, ring, [low[0] for low in lows], [low[1] for low in lows])
    return result.T


def solution(mesh):
    both = ("leaf", "sub")
    return jax.shard_map(
        on_device,
        mesh=mesh,
        in_specs=(
            P(None, both),
            P(both, None),
            P(both, None, None),
            P(both, None, None, None),
            P(both, None, None, None),
            P(),
            P(),
        ),
        out_specs=P(both, None),
        check_vma=False,
    )
```
